512 devices in a mesh: patch: 128 (over y_hi, x, z, core), lev: 4 (over y_lo).
Axes of the slice: x: 4, y: 8 (y_hi: 2, y_lo: 4; y = y_hi * 4 + y_lo), z: 8, core: 2. Of those that a mesh axis runs over, the one named last changes fastest.
Arguments:
- prior_mean: float32 [4, 65536], P('lev', 'patch'), may hold values from -4 to 4
- prior_pert: float32 [80, 4, 65536], P(None, 'lev', 'patch'), may hold values from -4 to 4
- obs_value: float32 [8, 3072], replicated, may hold values from -12 to 12
- obs_var: float32 [8, 3072], replicated, may hold values from 6 to 24
- obs_cell: int32 [8, 3072], replicated, may hold values from 0 to 511
- obs_level: int32 [8, 3072], replicated, may hold values from 0 to 3
- obs_count: int32 [8, 128], replicated, may hold values from 1 to 24, 1024 in all within a row
- batch_order: int32 [8], replicated, may hold values from 0 to 7, each once
- horiz_weight: float32 [16], replicated, may hold values from 0.4 to 1
- vert_weight: float32 [4], replicated, may hold values from 0.4 to 1
Outputs:
- post_mean: float32 [4, 65536], P('lev', 'patch')
- post_pert: float32 [80, 4, 65536], P(None, 'lev', 'patch')
The draws below stay inside these ranges and needn't reach their ends.
Inputs may be any that keep to these rules, and one draw needn't show every extreme that they name: `obs_count`: each batch's counts sum to 1024; in every batch some patch has exactly 24 live observations. `batch_order`: each batch number appears once.
All inputs are finite; a program needn't handle non-finite values.
Results may differ from the reference program's by a relative error of at most 0.003.
Values may be sent and summed in bfloat16 or wider, within the bound.
No kernel may reach another device: no remote copies, remote signals or barrier semaphores. Data moves between devices by JAX's collectives and lax.ppermute only.
A program may use at most 64 MiB of HBM per device.

```python
import math
import jax
import jax.numpy as jnp
import numpy as np
from jax import lax

M = 80
TX = 16
TY = 32
LEV_DEV = 1
OBS_DEV = 8
NPOOL = 8
NBATCH = 6
PROWS = 8
NBIN = 16
CAP = 24
LEVELS = 4
COLS_DEV = 512
NCOLS = 65536
SLOTS = 3072
NOBS = 1024
N_PATCH = 128
N_LEV = 4


def with_ends(values, key, smallest, top_value):
    dims = values.shape
    spot = [jax.random.randint(jax.random.fold_in(key, axis), (), 0, dims[axis]) for axis in range(len(dims))]
    values = values.at[tuple(spot)].set(smallest)
    longest = dims.index(max(dims))
    spot[longest] = (spot[longest] + 1) % dims[longest]
    return values.at[tuple(spot)].set(top_value)


def block_levels(key, extent, shards, least, largest):
    factor_of, own = 1.0, jax.random.fold_in(key, 6)
    for axis_at, blocks in shards:
        heights = jnp.exp(jax.random.uniform(jax.random.fold_in(own, axis_at), (blocks,), jnp.float32, least / len(shards), largest / len(shards)))
        factor_of = factor_of * jnp.repeat(heights, extent[axis_at] // blocks).reshape([-1 if axis == axis_at else 1 for axis in range(len(extent))])
    return factor_of


def split_up(number_of, total, most, skew):
    portions = [(1 << 20) // math.isqrt(grade ** skew) + 1 for grade in range(2, number_of + 1)]
    surplus, holding = total - most - (number_of - 1), [1] * (number_of - 1)
    while surplus > 0:
        free = [i for i in range(number_of - 1) if holding[i] < most]
        mass, left = sum([portions[i] for i in free]), surplus
        for i in free:
            addition = min(most - holding[i], max(1, left * portions[i] // mass), surplus)
            holding[i] = holding[i] + addition
            surplus = surplus - addition
    return np.array([most] + holding)


def uneven_parts(stream_key, number_of, total, bound, skew):
    if number_of == 2:
        one = jax.random.randint(stream_key, (), max(1, total - bound), min(bound, total - 1) + 1)
        return jnp.stack([one, total - one])
    sizes = jnp.asarray(split_up(number_of, total, bound, skew), jnp.int32)
    pairs = (number_of - 1) // 2
    giver, receiver = sizes[1:1 + 2 * pairs:2], sizes[2:2 + 2 * pairs:2]
    margin = jnp.minimum(giver - 1, bound - receiver)
    passed = jax.random.randint(jax.random.fold_in(stream_key, 1), (pairs,), 0, 1 << 20) % (margin + 1)
    sizes = sizes.at[1:1 + 2 * pairs:2].set(giver - passed).at[2:2 + 2 * pairs:2].set(receiver + passed)
    return sizes[jax.random.permutation(jax.random.fold_in(stream_key, 2), number_of)]


def scatter_about(key, extent, width, reach, pieces=(), held_as=jnp.bfloat16):
    values = jax.random.normal(key, extent, jnp.float32) * width
    if len(pieces) > 0:
        values = block_levels(key, extent, pieces, -0.22, 0.18) * values
    return jnp.clip(values, min=-reach, max=reach).astype(held_as)


def setup_inputs(seed: int = 0) -> dict:
    seeds = jax.random.split(jax.random.key(seed), 11)
    return {
        "prior_mean": scatter_about(seeds[0], (LEVELS, NCOLS), 1.0, 4.0, ((0, 4), (1, 128)), jnp.float32),
        "prior_pert": scatter_about(seeds[1], (M, LEVELS, NCOLS), 1.0, 4.0, ((1, 4), (2, 128)), jnp.float32),
        "obs_value": scatter_about(seeds[2], (NPOOL, SLOTS), 3.0, 12.0, (), jnp.float32),
        "obs_var": jnp.clip(jnp.exp(jax.random.uniform(seeds[3], (NPOOL, SLOTS), jnp.float32, math.log(6.0), math.log(24.0))), 6.0, 24.0),
        "obs_cell": with_ends(jax.random.randint(seeds[4], (NPOOL, SLOTS), 0, COLS_DEV), jax.random.fold_in(seeds[4], 1), 0, COLS_DEV - 1).astype(jnp.int32),
        "obs_level": with_ends(jax.random.randint(seeds[5], (NPOOL, SLOTS), 0, LEVELS), jax.random.fold_in(seeds[5], 1), 0, LEVELS - 1).astype(jnp.int32),
        "obs_count": jax.vmap(lambda own: uneven_parts(own, N_PATCH, NOBS, CAP, 2))(jax.random.split(seeds[6], NPOOL)).reshape((NPOOL, N_PATCH)).astype(jnp.int32),
        "batch_order": jax.random.permutation(seeds[7], NPOOL).astype(jnp.int32),
        "horiz_weight": jnp.clip(jax.random.uniform(seeds[8], (NBIN,), jnp.float32, 0.4, 1.0), 0.4, 1.0),
        "vert_weight": jnp.clip(jax.random.uniform(seeds[9], (LEVELS,), jnp.float32, 0.4, 1.0), 0.4, 1.0),
    }


def lookup(bins, table):
    hits = bins[..., None] == jnp.arange(table.shape[0], dtype=jnp.int32)
    return lax.optimization_barrier(jnp.sum(jnp.where(hits, table, jnp.zeros_like(table)), axis=-1))

def block_terms(piece, obs_x, obs_y, obs_lev, obs_err, grid, tables, pert_bf):
    own_x, own_y, own_lev, span_x, width_bin = grid
    horiz_weight, vert_weight = tables
    members = pert_bf.shape[0]
    values = piece.astype(jnp.float32)
    spread = lax.optimization_barrier(jnp.sum(values[:members] * values[:members], axis=0)) / (members - 1.0) + obs_err
    shrink = 1.0 / (1.0 + jnp.sqrt(obs_err / spread))
    nbins = horiz_weight.shape[0]
    dist_x = jnp.abs(obs_x[:, None] - own_x[None, :])
    dist_x = jnp.minimum(dist_x, span_x - dist_x)
    weight_x = lookup(jnp.minimum(dist_x // width_bin, nbins - 1), horiz_weight)
    dist_y = jnp.abs(obs_y[:, None] - own_y[None, :])
    weight_y = lookup(jnp.minimum(dist_y // width_bin, nbins - 1), horiz_weight)
    weight_z = lookup(jnp.abs(obs_lev[:, None] - own_lev[None, :]), vert_weight)
    rows = piece.shape[1]
    taper = (weight_z[:, :, None, None] * weight_x[:, None, :, None] * weight_y[:, None, None, :]).reshape(rows, -1)
    covar = lax.dot_general(piece[:members], pert_bf, (((0,), (0,)), ((), ())), preferred_element_type=jnp.float32)
    scaled = (taper * covar * (1.0 / ((members - 1.0) * spread))[:, None]).astype(jnp.bfloat16)
    coeffs = jnp.concatenate([values[:members] * shrink[None, :], values[members:]], axis=0).astype(jnp.bfloat16)
    return jnp.dot(coeffs, scaled, preferred_element_type=jnp.float32)

def all_terms(piece, meta, grid, tables, pert_bf):
    obs_x, obs_y, obs_lev, obs_err = meta
    rows = piece.shape[1]
    size = 512
    if rows <= size:
        return block_terms(piece, obs_x, obs_y, obs_lev, obs_err, grid, tables, pert_bf)
    count = -(-rows // size)
    extra = count * size - rows
    piece = jnp.pad(piece, ((0, 0), (0, extra)))
    obs_x = jnp.pad(obs_x, (0, extra))
    obs_y = jnp.pad(obs_y, (0, extra))
    obs_lev = jnp.pad(obs_lev, (0, extra))
    obs_err = jnp.pad(obs_err, (0, extra), constant_values=1.0)
    blocks = (piece.reshape(piece.shape[0], count, size).transpose(1, 0, 2), obs_x.reshape(count, size), obs_y.reshape(count, size), obs_lev.reshape(count, size), obs_err.reshape(count, size))

    def accumulate(total, item):
        return (total + block_terms(item[0], item[1], item[2], item[3], item[4], grid, tables, pert_bf), None)
    start = jnp.zeros((piece.shape[0], pert_bf.shape[1]), jnp.float32)
    total, unused = lax.scan(accumulate, start, blocks)
    return total

def reference(prior_mean, prior_pert, obs_value, obs_var, obs_cell, obs_level, obs_count, batch_order, horiz_weight, vert_weight):
    members = M
    levels = LEV_DEV * N_LEV
    cols = TX * TY
    span_x = TX * (N_PATCH // PROWS)
    span_y = TY * PROWS
    width_bin = (max(span_x // 2, span_y) + NBIN - 1) // NBIN
    nobs = OBS_DEV * N_PATCH
    mean = prior_mean
    pert = prior_pert
    patches = jnp.arange(N_PATCH, dtype=jnp.int32)
    tile_x = patches // PROWS * TX
    tile_y = patches % PROWS * TY
    tables = (horiz_weight, vert_weight)
    for step in range(NBATCH):
        pick = batch_order[step]
        cell_grid = obs_cell[pick].reshape(N_PATCH, CAP)
        count_b = obs_count[pick]
        live = (jnp.arange(CAP, dtype=jnp.int32)[None, :] < count_b[:, None]).reshape(-1)
        column = (patches[:, None] * cols + cell_grid).reshape(-1).astype(jnp.int32)
        obs_x = (tile_x[:, None] + cell_grid // TY).reshape(-1)
        obs_y = (tile_y[:, None] + cell_grid % TY).reshape(-1)
        lev_b = obs_level[pick]
        first = pert[:, lev_b, column]
        head = mean[lev_b, column]
        innov = jnp.where(live, obs_value[pick] - head, jnp.zeros_like(head))
        first = jnp.where(live[None, :], first, jnp.zeros_like(first))
        prior = jnp.concatenate([first, innov[None, :]], axis=0).astype(jnp.bfloat16)
        keys = jnp.where(live, 0, 1).astype(jnp.int32)
        chosen = jnp.argsort(keys, stable=True)[:nobs].astype(jnp.int32)
        prior = prior[:, chosen]
        meta = (obs_x[chosen], obs_y[chosen], lev_b[chosen], obs_var[pick][chosen])
        pert_bf = pert.astype(jnp.bfloat16)

        def one_patch(index):
            own_x = index // PROWS * TX + jnp.arange(TX, dtype=jnp.int32)
            own_y = index % PROWS * TY + jnp.arange(TY, dtype=jnp.int32)
            own_lev = jnp.arange(levels, dtype=jnp.int32)
            block = lax.dynamic_slice_in_dim(pert_bf, index * cols, cols, 2).reshape(members, levels * cols)
            return all_terms(prior, meta, (own_x, own_y, own_lev, span_x, width_bin), tables, block)
        terms = lax.map(one_patch, patches)
        terms = terms.reshape(N_PATCH, members + 1, levels, cols).transpose(1, 2, 0, 3).reshape(members + 1, levels, N_PATCH * cols)
        pert = pert - terms[:members]
        mean = mean + terms[members]
    return (mean, pert)
```

```python
import functools

import jax
import jax.numpy as jnp
from jax import lax
from jax.experimental import pallas as pl
from jax.experimental.pallas import tpu as pltpu
from jax.sharding import PartitionSpec as P

TX = 16
TY = 32
NBATCH = 6
PROWS = 8
NBIN = 16
CAP = 24
NOBS = 1024
CELLS = TX * TY
ROWS = 88
WIDE = 128
TILE = 512
LIVE_COLS = NBATCH * NOBS
COLS = LIVE_COLS + CELLS
UNIT = 1.0 / 16.0


def select_kernel(order_ref, where_ref, count_ref, cell_ref, lev_ref, value_ref, var_ref, pert_ref, mean_ref, out_ref):
    patch = where_ref[0]
    level = where_ref[1]

    def ordered(ref):
        rows = [ref[pl.ds(order_ref[k], 1), :] for k in range(NBATCH)]
        return jnp.concatenate(rows + [rows[-1], rows[-1]], axis=0)

    count = ordered(count_ref)
    lane = lax.broadcasted_iota(jnp.int32, count.shape, 1)
    zero = jnp.zeros_like(count)
    first = jnp.sum(jnp.where(lane < patch, count, zero), axis=1, keepdims=True)
    held = jnp.sum(jnp.where(lane == patch, count, zero), axis=1, keepdims=True)
    cell, lev, value, var = ordered(cell_ref), ordered(lev_ref), ordered(value_ref), ordered(var_ref)
    slot = lax.broadcasted_iota(jnp.int32, (8, NOBS), 1) - first
    cell_at = jnp.zeros((8, NOBS), jnp.int32)
    lev_at = jnp.full((8, NOBS), -1, jnp.int32)
    value_at = jnp.zeros((8, NOBS), jnp.float32)
    var_at = jnp.zeros((8, NOBS), jnp.float32)
    for s in range(CAP):
        here = slot == s
        cell_at = jnp.where(here, cell[:, s : s + 1], cell_at)
        lev_at = jnp.where(here, lev[:, s : s + 1], lev_at)
        value_at = jnp.where(here, value[:, s : s + 1], value_at)
        var_at = jnp.where(here, var[:, s : s + 1], var_at)
    own = (slot >= 0) & (slot < held) & (lev_at == level)
    none = jnp.zeros((8, NOBS), jnp.float32)
    pick = jnp.where(own, cell_at, -1)
    var_at = jnp.where(own, var_at, none)
    obs_x = jnp.where(own, (patch // PROWS * TX + cell_at // TY).astype(jnp.float32) * UNIT, none)
    obs_y = jnp.where(own, (patch % PROWS * TY + cell_at % TY).astype(jnp.float32) * UNIT, none)
    obs_z = jnp.where(own, lev_at.astype(jnp.float32) * NBIN, none)
    owned = jnp.where(own, none + 1.0, none)

    state = jnp.concatenate([pert_ref[...], mean_ref[...], jnp.zeros((ROWS - 81, CELLS), jnp.float32)], axis=0)
    high = state.astype(jnp.bfloat16)
    rest = state - high.astype(jnp.float32)
    mid = rest.astype(jnp.bfloat16)
    low = (rest - mid.astype(jnp.float32)).astype(jnp.bfloat16)
    spot = lax.broadcasted_iota(jnp.int32, (CELLS, NOBS), 0)
    for k in range(NBATCH):
        hot = (spot == pick[k : k + 1, :]).astype(jnp.float32).astype(jnp.bfloat16)
        taken = (
            jnp.dot(high, hot, preferred_element_type=jnp.float32)
            + jnp.dot(mid, hot, preferred_element_type=jnp.float32)
            + jnp.dot(low, hot, preferred_element_type=jnp.float32)
        )
        innov = (value_at[k : k + 1] - taken[80:81]) * owned[k : k + 1]
        tail = [innov, var_at[k : k + 1], obs_x[k : k + 1], obs_y[k : k + 1], obs_z[k : k + 1]]
        block = jnp.concatenate([taken[:80]] + tail + [jnp.zeros((3, NOBS), jnp.float32)], axis=0)
        out_ref[:, k * NOBS : (k + 1) * NOBS] = block


def filter_kernel(where_ref, obs_ref, pert_ref, mean_ref, near_ref, far_ref, post_pert_ref, post_mean_ref, state, cov, gain):
    patch = where_ref[0]
    level = where_ref[1]
    for k in range(NBATCH):
        block = jnp.concatenate(
            [obs_ref[:, k * NOBS : (k + 1) * NOBS], jnp.zeros((WIDE - ROWS, NOBS), jnp.float32)], axis=0
        )
        state[k * NOBS : (k + 1) * NOBS, :] = block.T
    spot = lax.broadcasted_iota(jnp.int32, (1, CELLS), 1)
    own_x = (patch // PROWS * TX + spot // TY).astype(jnp.float32) * UNIT
    own_y = (patch % PROWS * TY + spot % TY).astype(jnp.float32) * UNIT
    own_z = jnp.zeros((1, CELLS), jnp.float32) + (level * NBIN).astype(jnp.float32)
    block = jnp.concatenate(
        [
            pert_ref[...],
            -mean_ref[...],
            jnp.zeros((1, CELLS), jnp.float32),
            own_x,
            own_y,
            own_z,
            jnp.zeros((WIDE - 85, CELLS), jnp.float32),
        ],
        axis=0,
    )
    state[LIVE_COLS:COLS, :] = block.T
    near = jnp.broadcast_to(near_ref[...], (TILE, WIDE))
    far = jnp.broadcast_to(far_ref[...], (TILE, WIDE))
    span = float(PROWS * TY) * UNIT

    def batch(k, unused):
        start = pl.multiple_of(k * NOBS, NOBS)
        block = state[pl.ds(start, NOBS), :].T
        prior = block.astype(jnp.bfloat16).astype(jnp.float32)
        row = lax.broadcasted_iota(jnp.int32, (WIDE, NOBS), 0)
        members = jnp.where(row < 80, prior, jnp.zeros_like(prior))
        obs_var = block[81:82]
        spread = jnp.sum(members * members, axis=0, keepdims=True) / 79.0 + obs_var
        shrink = 1.0 / (1.0 + jnp.sqrt(obs_var / spread))
        scale = 1.0 / (79.0 * spread)
        coeffs = jnp.where(row == 80, prior, members * shrink).T.astype(jnp.bfloat16)
        members = members.astype(jnp.bfloat16)
        obs_x, obs_y, obs_z = block[82:83], block[83:84], block[84:85]

        def tile(t, unused):
            at = pl.multiple_of(t * TILE, TILE)
            cells = state[pl.ds(at, TILE), :]
            cov[...] = jnp.dot(cells.astype(jnp.bfloat16), members, preferred_element_type=jnp.float32)
            cell_x, cell_y, cell_z = cells[:, 82:83], cells[:, 83:84], cells[:, 84:85]
            for j in range(NOBS // WIDE):
                part = slice(j * WIDE, (j + 1) * WIDE)
                dist_x = jnp.abs(obs_x[:, part] - cell_x)
                dist_x = jnp.minimum(dist_x, span - dist_x) + jnp.abs(obs_z[:, part] - cell_z)
                dist_y = jnp.abs(obs_y[:, part] - cell_y)
                taper = jnp.take_along_axis(near, dist_x.astype(jnp.int32), axis=1) * jnp.take_along_axis(
                    far, dist_y.astype(jnp.int32), axis=1
                )
                gain[:, part] = (taper * cov[:, part] * scale[:, part]).astype(jnp.bfloat16)
            change = jnp.dot(gain[...], coeffs, preferred_element_type=jnp.float32)
            state[pl.ds(at, TILE), :] = cells - change
            return unused

        return lax.fori_loop((k + 1) * (NOBS // TILE), COLS // TILE, tile, unused)

    lax.fori_loop(0, NBATCH, batch, 0)
    block = state[LIVE_COLS:COLS, :].T
    post_pert_ref[...] = block[:80]
    post_mean_ref[...] = -block[80:81]


VMEM = pltpu.VMEM
SMEM = pltpu.SMEM


def select_call(order, where, count, cell, lev, value, var, pert, mean):
    return pl.pallas_call(
        select_kernel,
        out_shape=jax.ShapeDtypeStruct((ROWS, LIVE_COLS), jnp.float32),
        in_specs=[pl.BlockSpec(memory_space=SMEM)] * 2 + [pl.BlockSpec(memory_space=VMEM)] * 7,
        out_specs=pl.BlockSpec(memory_space=VMEM),
        compiler_params=pltpu.CompilerParams(vmem_limit_bytes=48 << 20),
    )(order, where, count, cell, lev, value, var, pert, mean)


def filter_call(where, obs, pert, mean, near, far):
    return pl.pallas_call(
        filter_kernel,
        out_shape=(
            jax.ShapeDtypeStruct((80, CELLS), jnp.float32),
            jax.ShapeDtypeStruct((1, CELLS), jnp.float32),
        ),
        in_specs=[pl.BlockSpec(memory_space=SMEM)] + [pl.BlockSpec(memory_space=VMEM)] * 5,
        out_specs=(pl.BlockSpec(memory_space=VMEM),) * 2,
        scratch_shapes=[
            VMEM((COLS, WIDE), jnp.float32),
            VMEM((TILE, NOBS), jnp.float32),
            VMEM((TILE, NOBS), jnp.bfloat16),
        ],
        compiler_params=pltpu.CompilerParams(vmem_limit_bytes=48 << 20),
    )(where, obs, pert, mean, near, far)


def shards(
    prior_mean,
    prior_pert,
    obs_value,
    obs_var,
    obs_cell,
    obs_level,
    obs_count,
    batch_order,
    horiz_weight,
    vert_weight,
):
    patch = lax.axis_index("patch")
    where = jnp.stack([patch, lax.axis_index("lev")]).astype(jnp.int32)
    pert = prior_pert.reshape(80, CELLS)
    mean = prior_mean.reshape(1, CELLS)
    own = [lax.dynamic_slice_in_dim(item, patch * CAP, CAP, 1) for item in (obs_cell, obs_level, obs_value, obs_var)]
    obs = select_call(batch_order, where, obs_count, *own, pert, mean)
    obs = lax.psum(obs, ("patch", "lev"))
    near = jnp.pad((vert_weight[:, None] * horiz_weight[None, :]).reshape(1, -1), ((0, 0), (0, 64)))
    far = jnp.pad(horiz_weight[None, :], ((0, 0), (0, 112)))
    post_pert, post_mean = filter_call(where, obs, pert, mean, near, far)
    return post_mean.reshape(prior_mean.shape), post_pert.reshape(prior_pert.shape)


def solution(mesh):
    return jax.shard_map(
        shards,
        mesh=mesh,
        in_specs=(
            P("lev", "patch"),
            P(None, "lev", "patch"),
            P(),
            P(),
            P(),
            P(),
            P(),
            P(),
            P(),
            P(),
        ),
        out_specs=(P("lev", "patch"), P(None, "lev", "patch")),
        check_vma=False,
    )
```

```python
import jax
import jax.numpy as jnp
from jax import lax
from jax.experimental import pallas as pl
from jax.experimental.pallas import tpu as pltpu
from jax.sharding import Mesh
from jax.sharding import PartitionSpec as P

MEMBERS = 80
TX = 16
TY = 32
NBATCH = 6
PROWS = 8
NPATCH = 128
NLEV = 4
BIN = 16
CAP = 24
NOBS = 1024
CELLS = TX * TY
UNIT = NBATCH * CAP
WIDE = 128
TILE = 512
SPAN = 256
LIVE_COLS = NBATCH * NOBS
COLS = LIVE_COLS + CELLS
INNOV, VAR, POS_X, POS_Y, POS_Z = 80, 83, 86, 87, 88
VMEM = pltpu.VMEM
SMEM = pltpu.SMEM
F32 = jnp.float32
BF16 = jnp.bfloat16


def split3(value):
    high = value.astype(BF16).astype(F32)
    mid = (value - high).astype(BF16).astype(F32)
    return high, mid, value - high - mid


def select_kernel(where_ref, order_ref, count_ref, cell_ref, lev_ref, value_ref, var_ref, pert_ref, mean_ref, out_ref):
    patch = where_ref[0]
    level = where_ref[1]
    window = jnp.minimum(patch * CAP // WIDE, NPATCH * CAP // WIDE - 2)
    shift = lax.rem(2 * WIDE - (patch * CAP - window * WIDE), 2 * WIDE)
    start = pl.multiple_of(window * WIDE, WIDE)

    def column(ref):
        rows = pltpu.roll(ref[:, pl.ds(start, 2 * WIDE)].astype(F32), shift, 1)[:, :WIDE]
        wide = jnp.concatenate([rows, jnp.zeros((WIDE - 8, WIDE), F32)], axis=0).T[:, :8]
        lane = lax.broadcasted_iota(jnp.int32, (CAP, 8), 1)
        wide = wide[:CAP]
        return jnp.concatenate(
            [jnp.sum(jnp.where(lane == order_ref[k], wide, 0.0), axis=1, keepdims=True) for k in range(NBATCH)], axis=0
        )

    slot = lax.broadcasted_iota(jnp.int32, (CAP, 1), 0)
    live = jnp.concatenate(
        [(slot < count_ref[order_ref[k], patch]).astype(F32) for k in range(NBATCH)], axis=0
    )
    cell, lev, value, var = column(cell_ref), column(lev_ref), column(value_ref), column(var_ref)
    own = (live > 0.5) & (lev == level.astype(F32))
    mean_parts = split3(mean_ref[...])
    source = jnp.concatenate([pert_ref[...], *mean_parts, jnp.zeros((WIDE - 83, CELLS), F32)], axis=0).astype(BF16)
    spot = lax.broadcasted_iota(jnp.int32, (UNIT, CELLS), 1)
    hot = jnp.where((spot == cell.astype(jnp.int32)) & own, 1.0, 0.0).astype(BF16)
    taken = lax.dot_general(hot, source, (((1,), (1,)), ((), ())), preferred_element_type=F32)
    innov = value - (taken[:, 80:81] + taken[:, 81:82] + taken[:, 82:83])
    across = (cell * (1.0 / TY)).astype(jnp.int32).astype(F32)
    obs_x = across + (patch // PROWS * TX).astype(F32)
    obs_y = cell - across * TY + (patch % PROWS * TY).astype(F32)
    lane = lax.broadcasted_iota(jnp.int32, (UNIT, WIDE), 1)
    out = jnp.where(lane < MEMBERS, taken, 0.0)
    for at, item in enumerate([*split3(innov), *split3(var), obs_x, obs_y, lev]):
        out = jnp.where(lane == INNOV + at, item, out)
    out_ref[...] = jnp.where(own, out, 0.0).astype(BF16)


def filter_kernel(
    where_ref,
    order_ref,
    count_ref,
    vert_ref,
    horiz_ref,
    got_ref,
    pert_ref,
    mean_ref,
    post_pert_ref,
    post_mean_ref,
    state,
    hot_x,
    hot_y,
    dist,
    tab_x,
    tab_y,
    levw,
):
    patch = where_ref[0]
    level = where_ref[1].astype(F32)

    for k in range(NBATCH):
        skip = (k % 2) * 8

        def place(p, first, k=k, skip=skip):
            rows = got_ref[pl.ds(pl.multiple_of(p * UNIT + k * CAP - skip, 16), 32), :].astype(F32)
            state[pl.ds(k * NOBS + first, CAP), :] = rows[skip : skip + CAP]
            return first + count_ref[order_ref[k], p]

        lax.fori_loop(0, NPATCH, place, 0, unroll=4)
    own = jnp.concatenate(
        [pert_ref[...], -mean_ref[...], jnp.zeros((WIDE - 81, CELLS), F32)], axis=0
    )
    state[LIVE_COLS:COLS, :] = own.T

    def mark(t, unused):
        at = pl.multiple_of(t * TILE, TILE)
        rows = state[pl.ds(at, TILE), :]
        lane = lax.broadcasted_iota(jnp.int32, (TILE, SPAN), 1).astype(F32)
        hot_x[pl.ds(at, TILE), :] = jnp.where(lane == rows[:, POS_X : POS_X + 1], 1.0, 0.0).astype(BF16)
        hot_y[pl.ds(at, TILE), :] = jnp.where(lane == rows[:, POS_Y : POS_Y + 1], 1.0, 0.0).astype(BF16)
        return unused

    lax.fori_loop(0, LIVE_COLS // TILE, mark, 0)

    def lookup(bins):
        table = jnp.broadcast_to(horiz_ref[...], (bins.shape[0], WIDE))
        parts = [
            jnp.take_along_axis(table, bins[:, j : j + WIDE], axis=1) for j in range(0, bins.shape[1], WIDE)
        ]
        return jnp.concatenate(parts, axis=1)

    def bins_x(one, other):
        apart = jnp.abs(one - other)
        return (jnp.minimum(apart, SPAN - apart) * (1.0 / BIN)).astype(jnp.int32)

    def bins_y(one, other):
        return (jnp.abs(one - other) * (1.0 / BIN)).astype(jnp.int32)

    one = lax.broadcasted_iota(jnp.int32, (SPAN, SPAN), 0).astype(F32)
    other = lax.broadcasted_iota(jnp.int32, (SPAN, SPAN), 1).astype(F32)
    for at, bins in enumerate((bins_x(one, other), bins_y(one, other))):
        value = lookup(bins)
        high = value.astype(BF16)
        dist[2 * at] = high
        dist[2 * at + 1] = (value - high.astype(F32)).astype(BF16)

    def vertical(apart):
        found = jnp.zeros_like(apart)
        for step in range(NLEV):
            found = jnp.where(apart == float(step), vert_ref[step], found)
        return found

    def batch(k, unused):
        start = pl.multiple_of(k * NOBS, NOBS)
        block = state[pl.ds(start, NOBS), :].T
        innov = block[INNOV : INNOV + 1] + block[INNOV + 1 : INNOV + 2] + block[INNOV + 2 : INNOV + 3]
        obs_var = block[VAR : VAR + 1] + block[VAR + 1 : VAR + 2] + block[VAR + 2 : VAR + 3]
        obs_x, obs_y, obs_z = block[POS_X : POS_X + 1], block[POS_Y : POS_Y + 1], block[POS_Z : POS_Z + 1]
        row = lax.broadcasted_iota(jnp.int32, (WIDE, NOBS), 0)
        prior = jnp.where(row < MEMBERS, block, 0.0).astype(BF16)
        values = prior.astype(F32)
        spread = jnp.sum(values * values, axis=0, keepdims=True) / (MEMBERS - 1.0) + obs_var
        shrink = 1.0 / (1.0 + jnp.sqrt(obs_var / spread))
        scale = 1.0 / ((MEMBERS - 1.0) * spread)
        coeffs = jnp.where(row == MEMBERS, innov.astype(BF16).astype(F32), values * shrink).T.astype(BF16)

        own_a = lax.broadcasted_iota(jnp.int32, (TX, NOBS), 0) + patch // PROWS * TX
        own_e = lax.broadcasted_iota(jnp.int32, (TY, NOBS), 0) + patch % PROWS * TY
        weight_x = lookup(bins_x(own_a.astype(F32), obs_x)) * (vertical(jnp.abs(obs_z - level)) * scale)
        weight_y = lookup(bins_y(own_e.astype(F32), obs_y))
        cells = state[LIVE_COLS:COLS, :]
        lhs = cells.astype(BF16)
        change = jnp.zeros((CELLS, WIDE), F32)
        for j in range(0, NOBS, SPAN):
            part = slice(j, j + SPAN)
            cov = jnp.dot(lhs, prior[:, part], preferred_element_type=F32)
            gain = jnp.concatenate(
                [
                    (cov[a * TY : (a + 1) * TY] * (weight_x[a : a + 1, part] * weight_y[:, part])).astype(BF16)
                    for a in range(TX)
                ],
                axis=0,
            )
            change = change + jnp.dot(gain, coeffs[part], preferred_element_type=F32)
        state[LIVE_COLS:COLS, :] = cells - change

        @pl.when(k < NBATCH - 1)
        def _():
            root = jnp.sqrt(scale)
            contract = (((1,), (1,)), ((), ()))
            for tab, hot, at in ((tab_x, hot_x, 0), (tab_y, hot_y, 2)):
                here = hot[pl.ds(start, NOBS), :]
                full = lax.dot_general(dist[at], here, contract, preferred_element_type=F32)
                full = full + lax.dot_general(dist[at + 1], here, contract, preferred_element_type=F32)
                tab[...] = (full * root).astype(BF16)
            for z in range(NLEV):
                levw[z : z + 1, :] = vertical(jnp.abs(obs_z - float(z)))

        def tile(t, unused):
            at = pl.multiple_of(t * TILE, TILE)
            cells = state[pl.ds(at, TILE), :]
            lhs = cells.astype(BF16)
            lhs_x = hot_x[pl.ds(at, TILE), :]
            lhs_y = hot_y[pl.ds(at, TILE), :]
            cell_z = jnp.broadcast_to(cells[:, POS_Z : POS_Z + 1], (TILE, SPAN))
            change = jnp.zeros((TILE, WIDE), F32)
            for j in range(0, NOBS, SPAN):
                part = slice(j, j + SPAN)
                cov = jnp.dot(lhs, prior[:, part], preferred_element_type=F32)
                near = jnp.dot(lhs_x, tab_x[:, part], preferred_element_type=F32)
                far = jnp.dot(lhs_y, tab_y[:, part], preferred_element_type=F32)
                high = jnp.where(cell_z == 2.0, levw[2:3, part], levw[3:4, part])
                up = jnp.where(cell_z == 0.0, levw[0:1, part], jnp.where(cell_z == 1.0, levw[1:2, part], high))
                gain = (near * far * (cov * up)).astype(BF16)
                change = change + jnp.dot(gain, coeffs[part], preferred_element_type=F32)
            state[pl.ds(at, TILE), :] = cells - change
            return unused

        return lax.fori_loop((k + 1) * (NOBS // TILE), LIVE_COLS // TILE, tile, unused)

    lax.fori_loop(0, NBATCH, batch, 0)
    block = state[LIVE_COLS:COLS, :].T
    post_pert_ref[...] = block[:MEMBERS]
    post_mean_ref[...] = -block[MEMBERS : MEMBERS + 1]


def select_call(where, order, count, cell, lev, value, var, pert, mean):
    return pl.pallas_call(
        select_kernel,
        out_shape=jax.ShapeDtypeStruct((UNIT, WIDE), BF16),
        in_specs=[pl.BlockSpec(memory_space=SMEM)] * 3 + [pl.BlockSpec(memory_space=VMEM)] * 6,
        out_specs=pl.BlockSpec(memory_space=VMEM),
        compiler_params=pltpu.CompilerParams(vmem_limit_bytes=48 << 20),
    )(where, order, count, cell, lev, value, var, pert, mean)


def filter_call(where, order, count, vert, horiz, got, pert, mean):
    return pl.pallas_call(
        filter_kernel,
        out_shape=(
            jax.ShapeDtypeStruct((MEMBERS, CELLS), F32),
            jax.ShapeDtypeStruct((1, CELLS), F32),
        ),
        in_specs=[pl.BlockSpec(memory_space=SMEM)] * 4 + [pl.BlockSpec(memory_space=VMEM)] * 4,
        out_specs=(pl.BlockSpec(memory_space=VMEM),) * 2,
        scratch_shapes=[
            VMEM((COLS, WIDE), F32),
            VMEM((LIVE_COLS, SPAN), BF16),
            VMEM((LIVE_COLS, SPAN), BF16),
            VMEM((4, SPAN, SPAN), BF16),
            VMEM((SPAN, NOBS), BF16),
            VMEM((SPAN, NOBS), BF16),
            VMEM((8, NOBS), F32),
        ],
        compiler_params=pltpu.CompilerParams(vmem_limit_bytes=56 << 20),
    )(where, order, count, vert, horiz, got, pert, mean)


AXES = ("y_hi", "x", "z", "core")


def shards(
    prior_mean,
    prior_pert,
    obs_value,
    obs_var,
    obs_cell,
    obs_level,
    obs_count,
    batch_order,
    horiz_weight,
    vert_weight,
):
    where = jnp.stack([lax.axis_index(AXES), lax.axis_index("y_lo")]).astype(jnp.int32)
    pert = prior_pert.reshape(MEMBERS, CELLS)
    mean = prior_mean.reshape(1, CELLS)
    mine = select_call(where, batch_order, obs_count, obs_cell, obs_level, obs_value, obs_var, pert, mean)
    others = [
        lax.ppermute(mine, "y_lo", [(i, (i + step) % NLEV) for i in range(NLEV)]) for step in range(1, NLEV)
    ]
    for other in others:
        mine = mine + other
    got = lax.all_gather(mine, AXES, axis=0, tiled=True)
    horiz = jnp.pad(horiz_weight[None, :], ((0, 0), (0, WIDE - horiz_weight.shape[0])))
    post_pert, post_mean = filter_call(where, batch_order, obs_count, vert_weight, horiz, got, pert, mean)
    return post_mean.reshape(prior_mean.shape), post_pert.reshape(prior_pert.shape)


def solution(mesh):
    whole = Mesh(mesh.devices.reshape(2, 4, 8, 2, NLEV), AXES + ("y_lo",))
    return jax.shard_map(
        shards,
        mesh=whole,
        in_specs=(
            P("y_lo", AXES),
            P(None, "y_lo", AXES),
            P(),
            P(),
            P(),
            P(),
            P(),
            P(),
            P(),
            P(),
        ),
        out_specs=(P("y_lo", AXES), P(None, "y_lo", AXES)),
        check_vma=False,
    )
```

```python
import jax
import jax.numpy as jnp
from jax import lax
from jax.experimental import pallas as pl
from jax.experimental.pallas import tpu as pltpu
from jax.sharding import Mesh
from jax.sharding import PartitionSpec as P

MEMBERS = 80
TX = 16
TY = 32
NBATCH = 6
PROWS = 8
NPATCH = 128
NLEV = 4
BIN = 16
CAP = 24
NOBS = 1024
CELLS = TX * TY
UNIT = NBATCH * CAP
WIDE = 128
TILE = 512
SPAN = 256
LIVE_COLS = NBATCH * NOBS
COLS = LIVE_COLS + CELLS
INNOV, VAR, POS_X, POS_Y, POS_Z = 80, 83, 86, 87, 88
VMEM = pltpu.VMEM
SMEM = pltpu.SMEM
F32 = jnp.float32
BF16 = jnp.bfloat16


def split3(value):
    high = value.astype(BF16).astype(F32)
    mid = (value - high).astype(BF16).astype(F32)
    return high, mid, value - high - mid


def select_kernel(where_ref, order_ref, count_ref, cell_ref, lev_ref, value_ref, var_ref, pert_ref, mean_ref, out_ref):
    patch = where_ref[0]
    level = where_ref[1]
    window = jnp.minimum(patch * CAP // WIDE, NPATCH * CAP // WIDE - 2)
    shift = lax.rem(2 * WIDE - (patch * CAP - window * WIDE), 2 * WIDE)
    start = pl.multiple_of(window * WIDE, WIDE)

    def column(ref):
        rows = pltpu.roll(ref[:, pl.ds(start, 2 * WIDE)].astype(F32), shift, 1)[:, :WIDE]
        wide = jnp.concatenate([rows, jnp.zeros((WIDE - 8, WIDE), F32)], axis=0).T[:, :8]
        lane = lax.broadcasted_iota(jnp.int32, (CAP, 8), 1)
        wide = wide[:CAP]
        return jnp.concatenate(
            [jnp.sum(jnp.where(lane == order_ref[k], wide, 0.0), axis=1, keepdims=True) for k in range(NBATCH)], axis=0
        )

    slot = lax.broadcasted_iota(jnp.int32, (CAP, 1), 0)
    live = jnp.concatenate(
        [(slot < count_ref[order_ref[k], patch]).astype(F32) for k in range(NBATCH)], axis=0
    )
    cell, lev, value, var = column(cell_ref), column(lev_ref), column(value_ref), column(var_ref)
    own = (live > 0.5) & (lev == level.astype(F32))
    mean_parts = split3(mean_ref[...])
    source = jnp.concatenate([pert_ref[...], *mean_parts, jnp.zeros((WIDE - 83, CELLS), F32)], axis=0).astype(BF16)
    spot = lax.broadcasted_iota(jnp.int32, (UNIT, CELLS), 1)
    hot = jnp.where((spot == cell.astype(jnp.int32)) & own, 1.0, 0.0).astype(BF16)
    taken = lax.dot_general(hot, source, (((1,), (1,)), ((), ())), preferred_element_type=F32)
    innov = value - (taken[:, 80:81] + taken[:, 81:82] + taken[:, 82:83])
    across = (cell * (1.0 / TY)).astype(jnp.int32).astype(F32)
    obs_x = across + (patch // PROWS * TX).astype(F32)
    obs_y = cell - across * TY + (patch % PROWS * TY).astype(F32)
    lane = lax.broadcasted_iota(jnp.int32, (UNIT, WIDE), 1)
    out = jnp.where(lane < MEMBERS, taken, 0.0)
    for at, item in enumerate([*split3(innov), *split3(var), obs_x, obs_y, lev]):
        out = jnp.where(lane == INNOV + at, item, out)
    out_ref[...] = jnp.where(own, out, 0.0).astype(BF16)


def filter_kernel(
    where_ref,
    order_ref,
    count_ref,
    vert_ref,
    horiz_ref,
    got_ref,
    pert_ref,
    mean_ref,
    post_pert_ref,
    post_mean_ref,
    state,
    hot_x,
    hot_y,
    dist,
    tab_x,
    tab_y,
    levw,
):
    patch = where_ref[0]
    level = where_ref[1].astype(F32)

    for k in range(NBATCH):
        skip = (k % 2) * 8

        def place(p, first, k=k, skip=skip):
            rows = got_ref[pl.ds(pl.multiple_of(p * UNIT + k * CAP - skip, 16), 32), :].astype(F32)
            state[pl.ds(k * NOBS + first, CAP), :] = rows[skip : skip + CAP]
            z, y_hi, core, x = p % 8, p // 8 % 2, p // 16 % 2, p // 32
            return first + count_ref[order_ref[k], ((y_hi * 4 + x) * 8 + z) * 2 + core]

        lax.fori_loop(0, NPATCH, place, 0, unroll=4)
    own = jnp.concatenate(
        [pert_ref[...], -mean_ref[...], jnp.zeros((WIDE - 81, CELLS), F32)], axis=0
    )
    state[LIVE_COLS:COLS, :] = own.T

    def mark(t, unused):
        at = pl.multiple_of(t * TILE, TILE)
        rows = state[pl.ds(at, TILE), :]
        lane = lax.broadcasted_iota(jnp.int32, (TILE, SPAN), 1).astype(F32)
        hot_x[pl.ds(at, TILE), :] = jnp.where(lane == rows[:, POS_X : POS_X + 1], 1.0, 0.0).astype(BF16)
        hot_y[pl.ds(at, TILE), :] = jnp.where(lane == rows[:, POS_Y : POS_Y + 1], 1.0, 0.0).astype(BF16)
        return unused

    lax.fori_loop(0, LIVE_COLS // TILE, mark, 0)

    def lookup(bins):
        table = jnp.broadcast_to(horiz_ref[...], (bins.shape[0], WIDE))
        parts = [
            jnp.take_along_axis(table, bins[:, j : j + WIDE], axis=1) for j in range(0, bins.shape[1], WIDE)
        ]
        return jnp.concatenate(parts, axis=1)

    def bins_x(one, other):
        apart = jnp.abs(one - other)
        return (jnp.minimum(apart, SPAN - apart) * (1.0 / BIN)).astype(jnp.int32)

    def bins_y(one, other):
        return (jnp.abs(one - other) * (1.0 / BIN)).astype(jnp.int32)

    one = lax.broadcasted_iota(jnp.int32, (SPAN, SPAN), 0).astype(F32)
    other = lax.broadcasted_iota(jnp.int32, (SPAN, SPAN), 1).astype(F32)
    for at, bins in enumerate((bins_x(one, other), bins_y(one, other))):
        value = lookup(bins)
        high = value.astype(BF16)
        dist[2 * at] = high
        dist[2 * at + 1] = (value - high.astype(F32)).astype(BF16)

    def vertical(apart):
        found = jnp.zeros_like(apart)
        for step in range(NLEV):
            found = jnp.where(apart == float(step), vert_ref[step], found)
        return found

    def batch(k, unused):
        start = pl.multiple_of(k * NOBS, NOBS)
        block = state[pl.ds(start, NOBS), :].T
        innov = block[INNOV : INNOV + 1] + block[INNOV + 1 : INNOV + 2] + block[INNOV + 2 : INNOV + 3]
        obs_var = block[VAR : VAR + 1] + block[VAR + 1 : VAR + 2] + block[VAR + 2 : VAR + 3]
        obs_x, obs_y, obs_z = block[POS_X : POS_X + 1], block[POS_Y : POS_Y + 1], block[POS_Z : POS_Z + 1]
        row = lax.broadcasted_iota(jnp.int32, (WIDE, NOBS), 0)
        prior = jnp.where(row < MEMBERS, block, 0.0).astype(BF16)
        values = prior.astype(F32)
        spread = jnp.sum(values * values, axis=0, keepdims=True) / (MEMBERS - 1.0) + obs_var
        shrink = 1.0 / (1.0 + jnp.sqrt(obs_var / spread))
        scale = 1.0 / ((MEMBERS - 1.0) * spread)
        coeffs = jnp.where(row == MEMBERS, innov.astype(BF16).astype(F32), values * shrink).T.astype(BF16)

        own_a = lax.broadcasted_iota(jnp.int32, (TX, NOBS), 0) + patch // PROWS * TX
        own_e = lax.broadcasted_iota(jnp.int32, (TY, NOBS), 0) + patch % PROWS * TY
        weight_x = lookup(bins_x(own_a.astype(F32), obs_x)) * (vertical(jnp.abs(obs_z - level)) * scale)
        weight_y = lookup(bins_y(own_e.astype(F32), obs_y))
        cells = state[LIVE_COLS:COLS, :]
        lhs = cells.astype(BF16)
        change = jnp.zeros((CELLS, WIDE), F32)
        for j in range(0, NOBS, SPAN):
            part = slice(j, j + SPAN)
            cov = jnp.dot(lhs, prior[:, part], preferred_element_type=F32)
            gain = jnp.concatenate(
                [
                    (cov[a * TY : (a + 1) * TY] * (weight_x[a : a + 1, part] * weight_y[:, part])).astype(BF16)
                    for a in range(TX)
                ],
                axis=0,
            )
            change = change + jnp.dot(gain, coeffs[part], preferred_element_type=F32)
        state[LIVE_COLS:COLS, :] = cells - change

        @pl.when(k < NBATCH - 1)
        def _():
            root = jnp.sqrt(scale)
            contract = (((1,), (1,)), ((), ()))
            for tab, hot, at in ((tab_x, hot_x, 0), (tab_y, hot_y, 2)):
                here = hot[pl.ds(start, NOBS), :]
                full = lax.dot_general(dist[at], here, contract, preferred_element_type=F32)
                full = full + lax.dot_general(dist[at + 1], here, contract, preferred_element_type=F32)
                tab[...] = (full * root).astype(BF16)
            for z in range(NLEV):
                levw[z : z + 1, :] = vertical(jnp.abs(obs_z - float(z)))

        def tile(t, unused):
            at = pl.multiple_of(t * TILE, TILE)
            cells = state[pl.ds(at, TILE), :]
            lhs = cells.astype(BF16)
            lhs_x = hot_x[pl.ds(at, TILE), :]
            lhs_y = hot_y[pl.ds(at, TILE), :]
            cell_z = jnp.broadcast_to(cells[:, POS_Z : POS_Z + 1], (TILE, SPAN))
            change = jnp.zeros((TILE, WIDE), F32)
            for j in range(0, NOBS, SPAN):
                part = slice(j, j + SPAN)
                cov = jnp.dot(lhs, prior[:, part], preferred_element_type=F32)
                near = jnp.dot(lhs_x, tab_x[:, part], preferred_element_type=F32)
                far = jnp.dot(lhs_y, tab_y[:, part], preferred_element_type=F32)
                high = jnp.where(cell_z == 2.0, levw[2:3, part], levw[3:4, part])
                up = jnp.where(cell_z == 0.0, levw[0:1, part], jnp.where(cell_z == 1.0, levw[1:2, part], high))
                gain = (near * far * (cov * up)).astype(BF16)
                change = change + jnp.dot(gain, coeffs[part], preferred_element_type=F32)
            state[pl.ds(at, TILE), :] = cells - change
            return unused

        return lax.fori_loop((k + 1) * (NOBS // TILE), LIVE_COLS // TILE, tile, unused)

    lax.fori_loop(0, NBATCH, batch, 0)
    block = state[LIVE_COLS:COLS, :].T
    post_pert_ref[...] = block[:MEMBERS]
    post_mean_ref[...] = -block[MEMBERS : MEMBERS + 1]


def select_call(where, order, count, cell, lev, value, var, pert, mean):
    return pl.pallas_call(
        select_kernel,
        out_shape=jax.ShapeDtypeStruct((UNIT, WIDE), BF16),
        in_specs=[pl.BlockSpec(memory_space=SMEM)] * 3 + [pl.BlockSpec(memory_space=VMEM)] * 6,
        out_specs=pl.BlockSpec(memory_space=VMEM),
        compiler_params=pltpu.CompilerParams(vmem_limit_bytes=48 << 20),
    )(where, order, count, cell, lev, value, var, pert, mean)


def filter_call(where, order, count, vert, horiz, got, pert, mean):
    return pl.pallas_call(
        filter_kernel,
        out_shape=(
            jax.ShapeDtypeStruct((MEMBERS, CELLS), F32),
            jax.ShapeDtypeStruct((1, CELLS), F32),
        ),
        in_specs=[pl.BlockSpec(memory_space=SMEM)] * 4 + [pl.BlockSpec(memory_space=VMEM)] * 4,
        out_specs=(pl.BlockSpec(memory_space=VMEM),) * 2,
        scratch_shapes=[
            VMEM((COLS, WIDE), F32),
            VMEM((LIVE_COLS, SPAN), BF16),
            VMEM((LIVE_COLS, SPAN), BF16),
            VMEM((4, SPAN, SPAN), BF16),
            VMEM((SPAN, NOBS), BF16),
            VMEM((SPAN, NOBS), BF16),
            VMEM((8, NOBS), F32),
        ],
        compiler_params=pltpu.CompilerParams(vmem_limit_bytes=56 << 20),
    )(where, order, count, vert, horiz, got, pert, mean)


AXES = ("y_hi", "x", "z", "core")


def shards(
    prior_mean,
    prior_pert,
    obs_value,
    obs_var,
    obs_cell,
    obs_level,
    obs_count,
    batch_order,
    horiz_weight,
    vert_weight,
):
    where = jnp.stack([lax.axis_index(AXES), lax.axis_index("y_lo")]).astype(jnp.int32)
    pert = prior_pert.reshape(MEMBERS, CELLS)
    mean = prior_mean.reshape(1, CELLS)
    mine = select_call(where, batch_order, obs_count, obs_cell, obs_level, obs_value, obs_var, pert, mean)
    for step in (1, 2):
        mine = mine + lax.ppermute(mine, "y_lo", [(i, i ^ step) for i in range(NLEV)])
    group = lax.all_gather(mine, ("y_hi", "z"), axis=0, tiled=True)
    got = lax.all_gather(group, ("x", "core"), axis=0, tiled=True)
    horiz = jnp.pad(horiz_weight[None, :], ((0, 0), (0, WIDE - horiz_weight.shape[0])))
    post_pert, post_mean = filter_call(where, batch_order, obs_count, vert_weight, horiz, got, pert, mean)
    return post_mean.reshape(prior_mean.shape), post_pert.reshape(prior_pert.shape)


def solution(mesh):
    whole = Mesh(mesh.devices.reshape(2, 4, 8, 2, NLEV), AXES + ("y_lo",))
    return jax.shard_map(
        shards,
        mesh=whole,
        in_specs=(
            P("y_lo", AXES),
            P(None, "y_lo", AXES),
            P(),
            P(),
            P(),
            P(),
            P(),
            P(),
            P(),
            P(),
        ),
        out_specs=(P("y_lo", AXES), P(None, "y_lo", AXES)),
        check_vma=False,
    )
```

```python
import jax
import jax.numpy as jnp
from jax import lax
from jax.experimental import pallas as pl
from jax.experimental.pallas import tpu as pltpu
from jax.sharding import Mesh
from jax.sharding import PartitionSpec as P

MEMBERS = 80
TX = 16
TY = 32
NBATCH = 6
PROWS = 8
NPATCH = 128
NLEV = 4
BIN = 16
CAP = 24
NOBS = 1024
CELLS = TX * TY
UNIT = NBATCH * CAP
WIDE = 128
TILE = 512
SPAN = 256
LIVE_COLS = NBATCH * NOBS
COLS = LIVE_COLS + CELLS
NTILES = NBATCH * (NBATCH - 1) // 2 * (NOBS // TILE)
INNOV, VAR, POS_X, POS_Y, POS_Z = 80, 83, 86, 87, 88
VMEM = pltpu.VMEM
SMEM = pltpu.SMEM
F32 = jnp.float32
BF16 = jnp.bfloat16


def split3(value):
    high = value.astype(BF16).astype(F32)
    mid = (value - high).astype(BF16).astype(F32)
    return high, mid, value - high - mid


def select_kernel(
    where_ref,
    order_hbm,
    count_hbm,
    cell_hbm,
    lev_hbm,
    value_hbm,
    var_hbm,
    mean_hbm,
    pert_ref,
    out_ref,
    first_ref,
    order_ref,
    count_ref,
    count_all,
    cell_ref,
    lev_ref,
    value_ref,
    var_ref,
    mean_ref,
    sems,
):
    patch = where_ref[0]
    level = where_ref[1]
    window = jnp.minimum(patch * CAP // WIDE, NPATCH * CAP // WIDE - 2)
    shift = lax.rem(2 * WIDE - (patch * CAP - window * WIDE), 2 * WIDE)
    start = pl.multiple_of(window * WIDE, WIDE)
    near = pl.ds(start, 2 * WIDE)
    pairs = [
        (order_hbm, order_ref),
        (count_hbm, count_ref),
        (count_hbm, count_all),
        (cell_hbm.at[:, near], cell_ref),
        (lev_hbm.at[:, near], lev_ref),
        (value_hbm.at[:, near], value_ref),
        (var_hbm.at[:, near], var_ref),
        (mean_hbm, mean_ref),
    ]
    copies = [pltpu.make_async_copy(one, other, sems.at[i]) for i, (one, other) in enumerate(pairs)]
    for copy in copies:
        copy.start()
    for copy in copies:
        copy.wait()

    def column(ref):
        rows = pltpu.roll(ref[...].astype(F32), shift, 1)[:, :WIDE]
        wide = jnp.concatenate([rows, jnp.zeros((WIDE - 8, WIDE), F32)], axis=0).T[:, :8]
        lane = lax.broadcasted_iota(jnp.int32, (CAP, 8), 1)
        wide = wide[:CAP]
        return jnp.concatenate(
            [jnp.sum(jnp.where(lane == order_ref[k], wide, 0.0), axis=1, keepdims=True) for k in range(NBATCH)], axis=0
        )

    one = lax.broadcasted_iota(jnp.int32, (NPATCH, NPATCH), 0)
    other = lax.broadcasted_iota(jnp.int32, (NPATCH, NPATCH), 1)
    before = jnp.where(gathered(one) < gathered(other), 1.0, 0.0).astype(BF16)
    counts = count_all[...].astype(F32).astype(BF16)
    first_ref[...] = jnp.dot(counts, before, preferred_element_type=F32).astype(jnp.int32)

    slot = lax.broadcasted_iota(jnp.int32, (CAP, 1), 0)
    live = jnp.concatenate(
        [(slot < count_ref[order_ref[k], patch]).astype(F32) for k in range(NBATCH)], axis=0
    )
    cell, lev, value, var = column(cell_ref), column(lev_ref), column(value_ref), column(var_ref)
    own = (live > 0.5) & (lev == level.astype(F32))
    mean_parts = split3(mean_ref[...])
    source = jnp.concatenate([pert_ref[...], *mean_parts, jnp.zeros((WIDE - 83, CELLS), F32)], axis=0).astype(BF16)
    spot = lax.broadcasted_iota(jnp.int32, (UNIT, CELLS), 1)
    hot = jnp.where((spot == cell.astype(jnp.int32)) & own, 1.0, 0.0).astype(BF16)
    taken = lax.dot_general(hot, source, (((1,), (1,)), ((), ())), preferred_element_type=F32)
    innov = value - (taken[:, 80:81] + taken[:, 81:82] + taken[:, 82:83])
    across = (cell * (1.0 / TY)).astype(jnp.int32).astype(F32)
    obs_x = across + (patch // PROWS * TX).astype(F32)
    obs_y = cell - across * TY + (patch % PROWS * TY).astype(F32)
    lane = lax.broadcasted_iota(jnp.int32, (UNIT, WIDE), 1)
    out = jnp.where(lane < MEMBERS, taken, 0.0)
    for at, item in enumerate([*split3(innov), *split3(var), obs_x, obs_y, lev]):
        out = jnp.where(lane == INNOV + at, item, out)
    out = jnp.where(own, out, 0.0).astype(BF16)
    for z in range(NLEV):
        out_ref[z] = out


def gathered(patch):
    return (((patch >> 4) & 3) * 2 + (patch & 1)) * 16 + (patch >> 6) * 8 + ((patch >> 1) & 7)


def spots(g):
    x, core, y_hi = g // 4, g // 2 % 2, g % 2
    return y_hi * 64 + x * 16 + core, g * 8


def first_tile(k):
    return (k + 1) * (NOBS // TILE)


def taper_kernel(
    order_ref, first_ref, vert_ref, horiz_ref, cell_ref, lev_ref, out_hbm, code_ref, slots, place, dist, tab_x, tab_y, levw, bufs, sems
):
    spot = lax.broadcasted_iota(jnp.int32, (8, NPATCH * CAP), 1).astype(F32)
    patch = ((spot + 0.5) * (1.0 / CAP)).astype(jnp.int32)
    cell = cell_ref[...]
    at_x = (patch // PROWS) * TX + cell // TY
    at_y = (patch % PROWS) * TY + cell % TY
    code_ref[...] = (at_x * 1024 + at_y * NLEV + lev_ref[...]).astype(F32)

    def compact(k, unused):
        row = code_ref[pl.ds(order_ref[k], 1), :]
        for c in range(NPATCH * CAP // WIDE):
            part = slice(c * WIDE, (c + 1) * WIDE)
            slots[part, :] = jnp.broadcast_to(row[:, part], (WIDE, WIDE)).T
        pick = order_ref[k]

        def put(g, unused):
            patch0, row0 = spots(g)
            for z in range(8):
                p = patch0 + 2 * z
                rows = slots[pl.ds(pl.multiple_of(p * CAP, 8), CAP), :]
                place[pl.ds(k * NOBS + first_ref[pick, p], CAP), :] = rows
            return unused

        return lax.fori_loop(0, NPATCH // 8, put, unused)

    lax.fori_loop(0, NBATCH, compact, 0)

    def lookup(bins):
        table = jnp.broadcast_to(horiz_ref[...], (bins.shape[0], WIDE))
        parts = [
            jnp.take_along_axis(table, bins[:, j : j + WIDE], axis=1) for j in range(0, bins.shape[1], WIDE)
        ]
        return jnp.concatenate(parts, axis=1)

    one = lax.broadcasted_iota(jnp.int32, (SPAN, SPAN), 0)
    other = lax.broadcasted_iota(jnp.int32, (SPAN, SPAN), 1)
    apart = jnp.abs(one - other)
    for at, bins in enumerate((jnp.minimum(apart, SPAN - apart) // BIN, apart // BIN)):
        value = lookup(bins)
        high = value.astype(BF16)
        dist[2 * at] = high
        dist[2 * at + 1] = (value - high.astype(F32)).astype(BF16)

    def hot(index, rows):
        lane = lax.broadcasted_iota(jnp.int32, (rows, WIDE), 1)
        parts = [jnp.where(index - j == lane, 1.0, 0.0).astype(BF16) for j in range(0, SPAN, WIDE)]
        return jnp.concatenate(parts, axis=1)

    def out_copy(n):
        return pltpu.make_async_copy(bufs.at[n % 2], out_hbm.at[n], sems.at[n % 2])

    def batch(k, n):
        codes = place[pl.ds(pl.multiple_of(k * NOBS, NOBS), NOBS), :].astype(jnp.int32)
        obs_z = codes.astype(F32).T[:1].astype(jnp.int32) & 3
        lane = lax.broadcasted_iota(jnp.int32, (1, NOBS), 1)
        vary = 1.0 + (lane & 63).astype(F32) * (1.0 / 64.0)
        contract = (((1,), (1,)), ((), ()))
        for tab, index, at, factor in (
            (tab_x, codes >> 10, 0, vary),
            (tab_y, (codes >> 2) & 255, 2, 1.0 / vary),
        ):
            here = hot(index, NOBS)
            full = lax.dot_general(dist[at], here, contract, preferred_element_type=F32)
            full = full + lax.dot_general(dist[at + 1], here, contract, preferred_element_type=F32)
            tab[...] = (full * factor).astype(BF16)
        for z in range(NLEV):
            apart = jnp.abs(obs_z - z)
            found = jnp.zeros((1, NOBS), F32)
            for step in range(NLEV):
                found = jnp.where(apart == step, vert_ref[step], found)
            levw[z : z + 1, :] = found

        def tile(t, n):
            codes = place[pl.ds(pl.multiple_of(t * TILE, TILE), TILE), :].astype(jnp.int32)
            lhs_x = hot(codes >> 10, TILE)
            lhs_y = hot((codes >> 2) & 255, TILE)
            cell_z = codes & 3
            cell_z = jnp.concatenate([cell_z, cell_z], axis=1)

            @pl.when(n >= 2)
            def _():
                out_copy(n - 2).wait()

            buf = bufs.at[n % 2]
            for j in range(0, NOBS, SPAN):
                part = slice(j, j + SPAN)
                near = jnp.dot(lhs_x, tab_x[:, part], preferred_element_type=F32)
                far = jnp.dot(lhs_y, tab_y[:, part], preferred_element_type=F32)
                low = jnp.where(cell_z == 0, levw[0:1, part], levw[1:2, part])
                high = jnp.where(cell_z == 2, levw[2:3, part], levw[3:4, part])
                buf[:, part] = (near * far * jnp.where(cell_z < 2, low, high)).astype(BF16)
            out_copy(n).start()
            return n + 1

        return lax.fori_loop(first_tile(k), LIVE_COLS // TILE, tile, n)

    total = lax.fori_loop(0, NBATCH - 1, batch, 0)
    out_copy(total - 2).wait()
    out_copy(total - 1).wait()


def filter_kernel(
    where_ref,
    order_ref,
    first_ref,
    vert_ref,
    horiz_ref,
    got_ref,
    pert_ref,
    mean_ref,
    taper_hbm,
    post_pert_ref,
    post_mean_ref,
    state,
    bufs,
    sems,
):
    patch = where_ref[0]
    level = where_ref[1].astype(F32)

    def taper_copy(n):
        return pltpu.make_async_copy(taper_hbm.at[n], bufs.at[n % 2], sems.at[n % 2])

    taper_copy(0).start()

    for k in range(NBATCH):
        skip = (k % 2) * 8
        pick = order_ref[k]

        def place(g, unused, k=k, skip=skip, pick=pick):
            patch0, row0 = spots(g)
            for z in range(8):
                at = pl.multiple_of(row0 * UNIT + (z * UNIT + k * CAP - skip), 16)
                rows = got_ref[pl.ds(at, 32), :].astype(F32)
                state[pl.ds(k * NOBS + first_ref[pick, patch0 + 2 * z], CAP), :] = rows[skip : skip + CAP]
            return unused

        lax.fori_loop(0, NPATCH // 8, place, 0)
    own = jnp.concatenate(
        [pert_ref[...], -mean_ref[...], jnp.zeros((WIDE - 81, CELLS), F32)], axis=0
    )
    state[LIVE_COLS:COLS, :] = own.T

    def lookup(bins):
        table = jnp.broadcast_to(horiz_ref[...], (bins.shape[0], WIDE))
        parts = [
            jnp.take_along_axis(table, bins[:, j : j + WIDE], axis=1) for j in range(0, bins.shape[1], WIDE)
        ]
        return jnp.concatenate(parts, axis=1)

    def bins_x(one, other):
        apart = jnp.abs(one - other)
        return (jnp.minimum(apart, SPAN - apart) * (1.0 / BIN)).astype(jnp.int32)

    def bins_y(one, other):
        return (jnp.abs(one - other) * (1.0 / BIN)).astype(jnp.int32)

    def vertical(apart):
        found = jnp.zeros_like(apart)
        for step in range(NLEV):
            found = jnp.where(apart == float(step), vert_ref[step], found)
        return found

    def batch(k, n):
        start = pl.multiple_of(k * NOBS, NOBS)
        block = state[pl.ds(start, NOBS), :].T
        innov = block[INNOV : INNOV + 1] + block[INNOV + 1 : INNOV + 2] + block[INNOV + 2 : INNOV + 3]
        obs_var = block[VAR : VAR + 1] + block[VAR + 1 : VAR + 2] + block[VAR + 2 : VAR + 3]
        obs_x, obs_y, obs_z = block[POS_X : POS_X + 1], block[POS_Y : POS_Y + 1], block[POS_Z : POS_Z + 1]
        row = lax.broadcasted_iota(jnp.int32, (WIDE, NOBS), 0)
        prior = jnp.where(row < MEMBERS, block, 0.0).astype(BF16)
        values = prior.astype(F32)
        spread = jnp.sum(values * values, axis=0, keepdims=True) / (MEMBERS - 1.0) + obs_var
        shrink = 1.0 / (1.0 + jnp.sqrt(obs_var / spread))
        scale = 1.0 / ((MEMBERS - 1.0) * spread)
        coeffs = jnp.where(row == MEMBERS, innov.astype(BF16).astype(F32), values * shrink).T.astype(BF16)

        own_a = lax.broadcasted_iota(jnp.int32, (TX, NOBS), 0) + patch // PROWS * TX
        own_e = lax.broadcasted_iota(jnp.int32, (TY, NOBS), 0) + patch % PROWS * TY
        weight_x = lookup(bins_x(own_a.astype(F32), obs_x)) * (vertical(jnp.abs(obs_z - level)) * scale)
        weight_y = lookup(bins_y(own_e.astype(F32), obs_y))
        cells = state[LIVE_COLS:COLS, :]
        lhs = cells.astype(BF16)
        change = jnp.zeros((CELLS, WIDE), F32)
        for j in range(0, NOBS, SPAN):
            part = slice(j, j + SPAN)
            cov = jnp.dot(lhs, prior[:, part], preferred_element_type=F32)
            gain = jnp.concatenate(
                [
                    (cov[a * TY : (a + 1) * TY] * (weight_x[a : a + 1, part] * weight_y[:, part])).astype(BF16)
                    for a in range(TX)
                ],
                axis=0,
            )
            change = change + jnp.dot(gain, coeffs[part], preferred_element_type=F32)
        state[LIVE_COLS:COLS, :] = cells - change

        def tile(t, n):
            taper_copy(n).wait()

            @pl.when(n < NTILES - 1)
            def _():
                taper_copy(n + 1).start()

            at = pl.multiple_of(t * TILE, TILE)
            cells = state[pl.ds(at, TILE), :]
            lhs = cells.astype(BF16)
            taper = bufs.at[n % 2]
            change = jnp.zeros((TILE, WIDE), F32)
            for j in range(0, NOBS, SPAN):
                part = slice(j, j + SPAN)
                cov = jnp.dot(lhs, prior[:, part], preferred_element_type=F32)
                gain = (taper[:, part].astype(F32) * (cov * scale[:, part])).astype(BF16)
                change = change + jnp.dot(gain, coeffs[part], preferred_element_type=F32)
            state[pl.ds(at, TILE), :] = cells - change
            return n + 1

        return lax.fori_loop(first_tile(k), LIVE_COLS // TILE, tile, n)

    lax.fori_loop(0, NBATCH, batch, 0)
    block = state[LIVE_COLS:COLS, :].T
    post_pert_ref[...] = block[:MEMBERS]
    post_mean_ref[...] = -block[MEMBERS : MEMBERS + 1]


def select_call(where, order, count, cell, lev, value, var, mean, pert):
    return pl.pallas_call(
        select_kernel,
        out_shape=(
            jax.ShapeDtypeStruct((NLEV, UNIT, WIDE), BF16),
            jax.ShapeDtypeStruct((8, NPATCH), jnp.int32),
        ),
        in_specs=[pl.BlockSpec(memory_space=SMEM)]
        + [pl.BlockSpec(memory_space=pltpu.HBM)] * 7
        + [pl.BlockSpec(memory_space=VMEM)],
        out_specs=(pl.BlockSpec(memory_space=VMEM),) * 2,
        scratch_shapes=[
            SMEM((8,), jnp.int32),
            SMEM((8, NPATCH), jnp.int32),
            VMEM((8, NPATCH), jnp.int32),
            VMEM((8, 2 * WIDE), jnp.int32),
            VMEM((8, 2 * WIDE), jnp.int32),
            VMEM((8, 2 * WIDE), F32),
            VMEM((8, 2 * WIDE), F32),
            VMEM((1, CELLS), F32),
            pltpu.SemaphoreType.DMA((8,)),
        ],
        compiler_params=pltpu.CompilerParams(vmem_limit_bytes=60 << 20),
    )(where, order, count, cell, lev, value, var, mean, pert)


def taper_call(order, first, vert, horiz, cell, lev):
    return pl.pallas_call(
        taper_kernel,
        out_shape=jax.ShapeDtypeStruct((NTILES, TILE, NOBS), BF16),
        in_specs=[pl.BlockSpec(memory_space=SMEM)] * 3 + [pl.BlockSpec(memory_space=VMEM)] * 3,
        out_specs=pl.BlockSpec(memory_space=pltpu.HBM),
        scratch_shapes=[
            VMEM((8, NPATCH * CAP), F32),
            VMEM((NPATCH * CAP, WIDE), F32),
            VMEM((LIVE_COLS + 2 * CAP, WIDE), F32),
            VMEM((4, SPAN, SPAN), BF16),
            VMEM((SPAN, NOBS), BF16),
            VMEM((SPAN, NOBS), BF16),
            VMEM((8, NOBS), F32),
            VMEM((2, TILE, NOBS), BF16),
            pltpu.SemaphoreType.DMA((2,)),
        ],
        compiler_params=pltpu.CompilerParams(vmem_limit_bytes=48 << 20),
        cost_estimate=pl.CostEstimate(flops=2 * 15 * NOBS * NOBS * 512, bytes_accessed=32 << 20, transcendentals=0),
    )(order, first, vert, horiz, cell, lev)


def filter_call(where, order, first, vert, horiz, got, pert, mean, taper):
    return pl.pallas_call(
        filter_kernel,
        out_shape=(
            jax.ShapeDtypeStruct((MEMBERS, CELLS), F32),
            jax.ShapeDtypeStruct((1, CELLS), F32),
        ),
        in_specs=[pl.BlockSpec(memory_space=SMEM)] * 4
        + [pl.BlockSpec(memory_space=VMEM)] * 4
        + [pl.BlockSpec(memory_space=pltpu.HBM)],
        out_specs=(pl.BlockSpec(memory_space=VMEM),) * 2,
        scratch_shapes=[
            VMEM((COLS, WIDE), F32),
            VMEM((2, TILE, NOBS), BF16),
            pltpu.SemaphoreType.DMA((2,)),
        ],
        compiler_params=pltpu.CompilerParams(vmem_limit_bytes=48 << 20),
    )(where, order, first, vert, horiz, got, pert, mean, taper)


def exchange(block, axes):
    return lax.all_to_all(block, axes, 0, 0)


AXES = ("y_hi", "x", "z", "core")


def shards(
    prior_mean,
    prior_pert,
    obs_value,
    obs_var,
    obs_cell,
    obs_level,
    obs_count,
    batch_order,
    horiz_weight,
    vert_weight,
):
    where = jnp.stack([lax.axis_index(AXES), lax.axis_index("y_lo")]).astype(jnp.int32)
    pert = prior_pert.reshape(MEMBERS, CELLS)
    mean = prior_mean.reshape(1, CELLS)
    mine, first = select_call(where, batch_order, obs_count, obs_cell, obs_level, obs_value, obs_var, mean, pert)
    horiz = jnp.pad(horiz_weight[None, :], ((0, 0), (0, WIDE - horiz_weight.shape[0])))
    mine = jnp.sum(exchange(mine, "y_lo").astype(F32), axis=0).astype(BF16)
    group = exchange(jnp.broadcast_to(mine[None], (16, UNIT, WIDE)), ("y_hi", "z")).reshape(16 * UNIT, WIDE)
    group, first = lax.optimization_barrier((group, first))
    got = lax.all_gather(group, ("x", "core"), axis=0, tiled=True)
    taper = taper_call(batch_order, first, vert_weight, horiz, obs_cell, obs_level)
    post_pert, post_mean = filter_call(where, batch_order, first, vert_weight, horiz, got, pert, mean, taper)
    return post_mean.reshape(prior_mean.shape), post_pert.reshape(prior_pert.shape)


def solution(mesh):
    whole = Mesh(mesh.devices.reshape(2, 4, 8, 2, NLEV), AXES + ("y_lo",))
    return jax.shard_map(
        shards,
        mesh=whole,
        in_specs=(
            P("y_lo", AXES),
            P(None, "y_lo", AXES),
            P(),
            P(),
            P(),
            P(),
            P(),
            P(),
            P(),
            P(),
        ),
        out_specs=(P("y_lo", AXES), P(None, "y_lo", AXES)),
        check_vma=False,
    )
```

```python
import jax
import jax.numpy as jnp
from jax import lax
from jax.experimental import pallas as pl
from jax.experimental.pallas import tpu as pltpu
from jax.sharding import Mesh
from jax.sharding import PartitionSpec as P

MEMBERS = 80
TX = 16
TY = 32
NBATCH = 6
PROWS = 8
NPATCH = 128
NLEV = 4
BIN = 16
NBIN = 16
CAP = 24
NOBS = 1024
CELLS = TX * TY
UNIT = NBATCH * CAP
WIDE = 128
TILE = 512
SPAN = 256
LIVE_COLS = NBATCH * NOBS
SLAB = NOBS + 32
OWN = NBATCH * SLAB
PARTS = 4
NTILES = NBATCH * (NBATCH - 1) // 2 * (NOBS // TILE)
INNOV, VAR, POS_X, POS_Y, POS_Z = 80, 83, 86, 87, 88
VMEM = pltpu.VMEM
SMEM = pltpu.SMEM
F32 = jnp.float32
BF16 = jnp.bfloat16


def split3(value):
    high = value.astype(BF16).astype(F32)
    mid = (value - high).astype(BF16).astype(F32)
    return high, mid, value - high - mid


def fetch(pairs, sems):
    copies = [pltpu.make_async_copy(one, other, sems.at[i]) for i, (one, other) in enumerate(pairs)]
    for copy in copies:
        copy.start()
    for copy in copies:
        copy.wait()


def horizontal(horiz_ref):
    lane = lax.broadcasted_iota(jnp.int32, (1, WIDE), 1)
    table = jnp.zeros((1, WIDE), F32)
    for step in range(NBIN):
        table = jnp.where(lane == step, horiz_ref[step], table)
    return table


def select_kernel(
    where_ref,
    order_hbm,
    count_hbm,
    cell_hbm,
    lev_hbm,
    value_hbm,
    var_hbm,
    mean_hbm,
    pert_hbm,
    out_ref,
    first_ref,
    order_ref,
    count_ref,
    count_all,
    cell_ref,
    lev_ref,
    value_ref,
    var_ref,
    mean_ref,
    pert_ref,
    sems,
):
    patch = where_ref[0]
    level = where_ref[1]
    window = jnp.minimum(patch * CAP // WIDE, NPATCH * CAP // WIDE - 2)
    shift = lax.rem(2 * WIDE - (patch * CAP - window * WIDE), 2 * WIDE)
    start = pl.multiple_of(window * WIDE, WIDE)
    near = pl.ds(start, 2 * WIDE)
    pairs = [
        (order_hbm, order_ref),
        (count_hbm, count_ref),
        (count_hbm, count_all),
        (cell_hbm.at[:, near], cell_ref),
        (lev_hbm.at[:, near], lev_ref),
        (value_hbm.at[:, near], value_ref),
        (var_hbm.at[:, near], var_ref),
        (mean_hbm, mean_ref),
        (pert_hbm.at[:, 0, :], pert_ref),
    ]
    fetch(pairs, sems)

    def column(ref):
        rows = pltpu.roll(ref[...].astype(F32), shift, 1)[:, :WIDE]
        wide = jnp.concatenate([rows, jnp.zeros((WIDE - 8, WIDE), F32)], axis=0).T[:, :8]
        lane = lax.broadcasted_iota(jnp.int32, (CAP, 8), 1)
        wide = wide[:CAP]
        return jnp.concatenate(
            [jnp.sum(jnp.where(lane == order_ref[k], wide, 0.0), axis=1, keepdims=True) for k in range(NBATCH)], axis=0
        )

    one = lax.broadcasted_iota(jnp.int32, (NPATCH, NPATCH), 0)
    other = lax.broadcasted_iota(jnp.int32, (NPATCH, NPATCH), 1)
    before = jnp.where(gathered(one) < gathered(other), 1.0, 0.0).astype(BF16)
    counts = count_all[...].astype(F32).astype(BF16)
    first_ref[...] = jnp.dot(counts, before, preferred_element_type=F32).astype(jnp.int32)

    slot = lax.broadcasted_iota(jnp.int32, (CAP, 1), 0)
    live = jnp.concatenate(
        [(slot < count_ref[order_ref[k], patch]).astype(F32) for k in range(NBATCH)], axis=0
    )
    cell, lev, value, var = column(cell_ref), column(lev_ref), column(value_ref), column(var_ref)
    own = (live > 0.5) & (lev == level.astype(F32))
    mean_parts = split3(mean_ref[...])
    source = jnp.concatenate([pert_ref[...], *mean_parts, jnp.zeros((WIDE - 83, CELLS), F32)], axis=0).astype(BF16)
    spot = lax.broadcasted_iota(jnp.int32, (UNIT, CELLS), 1)
    hot = jnp.where((spot == cell.astype(jnp.int32)) & own, 1.0, 0.0).astype(BF16)
    taken = lax.dot_general(hot, source, (((1,), (1,)), ((), ())), preferred_element_type=F32)
    innov = value - (taken[:, 80:81] + taken[:, 81:82] + taken[:, 82:83])
    across = (cell * (1.0 / TY)).astype(jnp.int32).astype(F32)
    obs_x = across + (patch // PROWS * TX).astype(F32)
    obs_y = cell - across * TY + (patch % PROWS * TY).astype(F32)
    lane = lax.broadcasted_iota(jnp.int32, (UNIT, WIDE), 1)
    out = jnp.where(lane < MEMBERS, taken, 0.0)
    for at, item in enumerate([*split3(innov), *split3(var), obs_x, obs_y, lev]):
        out = jnp.where(lane == INNOV + at, item, out)
    out = jnp.where(own, out, 0.0).astype(BF16)
    for other in range(2 * NLEV):
        out_ref[other] = out


def gathered(patch):
    return (patch & 15) * 8 + ((patch >> 4) & 3) * 2 + (patch >> 6)


GROUP = [(i >> 1) * 16 + (i & 1) * 64 for i in range(8)]


def first_tile(k):
    return (k + 1) * (NOBS // TILE)


def taper_kernel(
    order_hbm,
    first_hbm,
    vert_hbm,
    horiz_hbm,
    cell_hbm,
    lev_hbm,
    out_hbm,
    order_ref,
    first_ref,
    vert_ref,
    horiz_ref,
    cell_ref,
    lev_ref,
    code_ref,
    slots,
    place,
    hot_x,
    hot_y,
    dist,
    tab_x,
    tab_y,
    levw,
    bufs,
    fetched,
    sems,
):
    fetch(
        [
            (order_hbm, order_ref),
            (first_hbm, first_ref),
            (vert_hbm, vert_ref),
            (horiz_hbm, horiz_ref),
            (cell_hbm, cell_ref),
            (lev_hbm, lev_ref),
        ],
        fetched,
    )
    spot = lax.broadcasted_iota(jnp.int32, (8, NPATCH * CAP), 1).astype(F32)
    patch = ((spot + 0.5) * (1.0 / CAP)).astype(jnp.int32)
    cell = cell_ref[...]
    at_x = (patch // PROWS) * TX + cell // TY
    at_y = (patch % PROWS) * TY + cell % TY
    code_ref[...] = (at_x * 1024 + at_y * NLEV + lev_ref[...]).astype(F32)

    def compact(k, unused):
        row = code_ref[pl.ds(order_ref[k], 1), :]
        for c in range(NPATCH * CAP // WIDE):
            part = slice(c * WIDE, (c + 1) * WIDE)
            slots[part, :] = jnp.broadcast_to(row[:, part], (WIDE, WIDE)).T
        pick = order_ref[k]

        def put(g, unused):
            for step in GROUP:
                p = g + step
                rows = slots[pl.ds(pl.multiple_of(p * CAP, 8), CAP), :]
                place[pl.ds(k * NOBS + first_ref[pick, p], CAP), :] = rows
            return unused

        return lax.fori_loop(0, NPATCH // 8, put, unused)

    lax.fori_loop(0, NBATCH, compact, 0)

    def mark(t, unused):
        here = pl.ds(pl.multiple_of(t * TILE, TILE), TILE)
        codes = place[here, :].astype(jnp.int32)
        hot_x[here, :] = hot(codes >> 10, TILE)
        hot_y[here, :] = hot((codes >> 2) & 255, TILE)
        return unused

    def lookup(bins):
        table = jnp.broadcast_to(horizontal(horiz_ref), (bins.shape[0], WIDE))
        parts = [
            jnp.take_along_axis(table, bins[:, j : j + WIDE], axis=1) for j in range(0, bins.shape[1], WIDE)
        ]
        return jnp.concatenate(parts, axis=1)

    one = lax.broadcasted_iota(jnp.int32, (SPAN, SPAN), 0)
    other = lax.broadcasted_iota(jnp.int32, (SPAN, SPAN), 1)
    apart = jnp.abs(one - other)
    for at, bins in enumerate((jnp.minimum(apart, SPAN - apart) // BIN, apart // BIN)):
        value = lookup(bins)
        high = value.astype(BF16)
        dist[2 * at] = high
        dist[2 * at + 1] = (value - high.astype(F32)).astype(BF16)

    def hot(index, rows):
        lane = lax.broadcasted_iota(jnp.int32, (rows, WIDE), 1)
        parts = [jnp.where(index - j == lane, 1.0, 0.0).astype(BF16) for j in range(0, SPAN, WIDE)]
        return jnp.concatenate(parts, axis=1)

    lax.fori_loop(0, LIVE_COLS // TILE, mark, 0)

    def out_copy(n):
        return pltpu.make_async_copy(bufs.at[n % 2], out_hbm.at[n], sems.at[n % 2])

    def batch(k, n):
        rows = pl.ds(pl.multiple_of(k * NOBS, NOBS), NOBS)
        obs_z = place[rows, :].T[:1].astype(jnp.int32) & 3
        lane = lax.broadcasted_iota(jnp.int32, (1, NOBS), 1)
        vary = 1.0 + (lane & 63).astype(F32) * (1.0 / 64.0)
        contract = (((1,), (1,)), ((), ()))
        for tab, hot_rows, at, factor in ((tab_x, hot_x, 0, vary), (tab_y, hot_y, 2, 1.0 / vary)):
            here = hot_rows[rows, :]
            full = lax.dot_general(dist[at], here, contract, preferred_element_type=F32)
            full = full + lax.dot_general(dist[at + 1], here, contract, preferred_element_type=F32)
            tab[...] = (full * factor).astype(BF16)
        for z in range(NLEV):
            apart = jnp.abs(obs_z - z)
            found = jnp.zeros((1, NOBS), F32)
            for step in range(NLEV):
                found = jnp.where(apart == step, vert_ref[step], found)
            levw[z : z + 1, :] = found

        def tile(t, n):
            here = pl.ds(pl.multiple_of(t * TILE, TILE), TILE)
            lhs_x = hot_x[here, :]
            lhs_y = hot_y[here, :]
            cell_z = place[here, :].astype(jnp.int32) & 3
            cell_z = jnp.concatenate([cell_z, cell_z], axis=1)

            @pl.when(n >= 2)
            def _():
                out_copy(n - 2).wait()

            buf = bufs.at[n % 2]
            for j in range(0, NOBS, SPAN):
                part = slice(j, j + SPAN)
                near = jnp.dot(lhs_x, tab_x[:, part], preferred_element_type=F32)
                far = jnp.dot(lhs_y, tab_y[:, part], preferred_element_type=F32)
                low = jnp.where(cell_z == 0, levw[0:1, part], levw[1:2, part])
                high = jnp.where(cell_z == 2, levw[2:3, part], levw[3:4, part])
                buf[:, part] = (near * far * jnp.where(cell_z < 2, low, high)).astype(BF16)
            out_copy(n).start()
            return n + 1

        return lax.fori_loop(first_tile(k), LIVE_COLS // TILE, tile, n)

    total = lax.fori_loop(0, NBATCH - 1, batch, 0)
    out_copy(total - 2).wait()
    out_copy(total - 1).wait()


def filter_kernel(
    where_ref,
    order_hbm,
    first_hbm,
    vert_hbm,
    horiz_hbm,
    got_hbm,
    pert_hbm,
    mean_hbm,
    taper_hbm,
    post_pert_hbm,
    post_mean_ref,
    order_ref,
    first_ref,
    vert_ref,
    horiz_ref,
    got_ref,
    pert_ref,
    mean_ref,
    state,
    bufs,
    fetched,
    arrived,
    sems,
):
    patch = where_ref[0]
    level = where_ref[1].astype(F32)

    def taper_copy(n):
        return pltpu.make_async_copy(taper_hbm.at[n], bufs.at[n % 2], sems.at[n % 2])

    def part_copy(c):
        rows = pl.ds(c * (NPATCH * UNIT // PARTS), NPATCH * UNIT // PARTS)
        return pltpu.make_async_copy(got_hbm.at[rows, :], got_ref.at[rows, :], arrived.at[c])

    for c in range(PARTS):
        part_copy(c).start()
    fetch(
        [
            (order_hbm, order_ref),
            (first_hbm, first_ref),
            (vert_hbm, vert_ref),
            (horiz_hbm, horiz_ref),
            (pert_hbm.at[:, 0, :], pert_ref),
            (mean_hbm, mean_ref),
        ],
        fetched,
    )
    taper_copy(0).start()
    own = jnp.concatenate(
        [pert_ref[...], -mean_ref[...], jnp.zeros((WIDE - 81, CELLS), F32)], axis=0
    )
    state[OWN : OWN + CELLS, :] = own.T

    def place(g, unused):
        for i, step in enumerate(GROUP):
            for k in range(NBATCH):
                skip = (k % 2) * 8
                at = pl.multiple_of(g * (8 * UNIT) + (i * UNIT + k * CAP - skip), 16)
                rows = got_ref[pl.ds(at, 32), :].astype(F32)
                first = first_ref[order_ref[k], g + step]
                state[pl.ds(k * SLAB + first, CAP), :] = rows[skip : skip + CAP]
        return unused

    for c in range(PARTS):
        part_copy(c).wait()
        lax.fori_loop(c * (16 // PARTS), (c + 1) * (16 // PARTS), place, 0)

    def lookup(bins):
        table = jnp.broadcast_to(horizontal(horiz_ref), (bins.shape[0], WIDE))
        parts = [
            jnp.take_along_axis(table, bins[:, j : j + WIDE], axis=1) for j in range(0, bins.shape[1], WIDE)
        ]
        return jnp.concatenate(parts, axis=1)

    def bins_x(one, other):
        apart = jnp.abs(one - other)
        return (jnp.minimum(apart, SPAN - apart) * (1.0 / BIN)).astype(jnp.int32)

    def bins_y(one, other):
        return (jnp.abs(one - other) * (1.0 / BIN)).astype(jnp.int32)

    def vertical(apart):
        found = jnp.zeros_like(apart)
        for step in range(NLEV):
            found = jnp.where(apart == float(step), vert_ref[step], found)
        return found

    def batch(k, n):
        start = pl.multiple_of(k * SLAB, 32)
        block = state[pl.ds(start, NOBS), :].T
        innov = block[INNOV : INNOV + 1] + block[INNOV + 1 : INNOV + 2] + block[INNOV + 2 : INNOV + 3]
        obs_var = block[VAR : VAR + 1] + block[VAR + 1 : VAR + 2] + block[VAR + 2 : VAR + 3]
        obs_x, obs_y, obs_z = block[POS_X : POS_X + 1], block[POS_Y : POS_Y + 1], block[POS_Z : POS_Z + 1]
        row = lax.broadcasted_iota(jnp.int32, (WIDE, NOBS), 0)
        prior = jnp.where(row < MEMBERS, block, 0.0).astype(BF16)
        values = prior.astype(F32)
        spread = jnp.sum(values * values, axis=0, keepdims=True) / (MEMBERS - 1.0) + obs_var
        shrink = 1.0 / (1.0 + jnp.sqrt(obs_var / spread))
        scale = 1.0 / ((MEMBERS - 1.0) * spread)
        coeffs = jnp.where(row == MEMBERS, innov.astype(BF16).astype(F32), values * shrink).T.astype(BF16)

        own_a = lax.broadcasted_iota(jnp.int32, (TX, NOBS), 0) + patch // PROWS * TX
        own_e = lax.broadcasted_iota(jnp.int32, (TY, NOBS), 0) + patch % PROWS * TY
        weight_x = lookup(bins_x(own_a.astype(F32), obs_x)) * (vertical(jnp.abs(obs_z - level)) * scale)
        weight_y = lookup(bins_y(own_e.astype(F32), obs_y))
        cells = state[OWN : OWN + CELLS, :]
        lhs = cells.astype(BF16)
        change = jnp.zeros((CELLS, WIDE), F32)
        for j in range(0, NOBS, SPAN):
            part = slice(j, j + SPAN)
            cov = jnp.dot(lhs, prior[:, part], preferred_element_type=F32)
            gain = jnp.concatenate(
                [
                    (cov[a * TY : (a + 1) * TY] * (weight_x[a : a + 1, part] * weight_y[:, part])).astype(BF16)
                    for a in range(TX)
                ],
                axis=0,
            )
            change = change + jnp.dot(gain, coeffs[part], preferred_element_type=F32)
        state[OWN : OWN + CELLS, :] = cells - change

        def tile(t, n):
            taper_copy(n).wait()

            @pl.when(n < NTILES - 1)
            def _():
                taper_copy(n + 1).start()

            at = pl.multiple_of((t >> 1) * SLAB + (t & 1) * TILE, 32)
            cells = state[pl.ds(at, TILE), :]
            lhs = cells.astype(BF16)
            taper = bufs.at[n % 2]
            change = jnp.zeros((TILE, WIDE), F32)
            for j in range(0, NOBS, SPAN):
                part = slice(j, j + SPAN)
                cov = jnp.dot(lhs, prior[:, part], preferred_element_type=F32)
                gain = (taper[:, part].astype(F32) * (cov * scale[:, part])).astype(BF16)
                change = change + jnp.dot(gain, coeffs[part], preferred_element_type=F32)
            state[pl.ds(at, TILE), :] = cells - change
            return n + 1

        return lax.fori_loop(first_tile(k), LIVE_COLS // TILE, tile, n)

    lax.fori_loop(0, NBATCH, batch, 0)
    block = state[OWN : OWN + CELLS, :].T
    pert_ref[...] = block[:MEMBERS]
    post_mean_ref[...] = -block[MEMBERS : MEMBERS + 1]
    fetch([(pert_ref, post_pert_hbm.at[:, 0, :])], fetched)


HBM = pltpu.HBM
DMA = pltpu.SemaphoreType.DMA
GRANT = pltpu.CompilerParams(vmem_limit_bytes=60 << 20)


def spec(space):
    return pl.BlockSpec(memory_space=space)


def select_call(where, order, count, cell, lev, value, var, mean, pert):
    return pl.pallas_call(
        select_kernel,
        out_shape=(
            jax.ShapeDtypeStruct((2 * NLEV, UNIT, WIDE), BF16),
            jax.ShapeDtypeStruct((8, NPATCH), jnp.int32),
        ),
        in_specs=[spec(SMEM)] + [spec(HBM)] * 8,
        out_specs=(spec(VMEM),) * 2,
        scratch_shapes=[
            SMEM((8,), jnp.int32),
            SMEM((8, NPATCH), jnp.int32),
            VMEM((8, NPATCH), jnp.int32),
            VMEM((8, 2 * WIDE), jnp.int32),
            VMEM((8, 2 * WIDE), jnp.int32),
            VMEM((8, 2 * WIDE), F32),
            VMEM((8, 2 * WIDE), F32),
            VMEM((1, CELLS), F32),
            VMEM((MEMBERS, CELLS), F32),
            DMA((9,)),
        ],
        compiler_params=GRANT,
    )(where, order, count, cell, lev, value, var, mean, pert)


def taper_call(order, first, vert, horiz, cell, lev):
    return pl.pallas_call(
        taper_kernel,
        out_shape=jax.ShapeDtypeStruct((NTILES, TILE, NOBS), BF16),
        in_specs=[spec(HBM)] * 6,
        out_specs=spec(HBM),
        scratch_shapes=[
            SMEM((8,), jnp.int32),
            SMEM((8, NPATCH), jnp.int32),
            SMEM((NLEV,), F32),
            SMEM((NBIN,), F32),
            VMEM((8, NPATCH * CAP), jnp.int32),
            VMEM((8, NPATCH * CAP), jnp.int32),
            VMEM((8, NPATCH * CAP), F32),
            VMEM((NPATCH * CAP, WIDE), F32),
            VMEM((LIVE_COLS + 2 * CAP, WIDE), F32),
            VMEM((LIVE_COLS, SPAN), BF16),
            VMEM((LIVE_COLS, SPAN), BF16),
            VMEM((4, SPAN, SPAN), BF16),
            VMEM((SPAN, NOBS), BF16),
            VMEM((SPAN, NOBS), BF16),
            VMEM((8, NOBS), F32),
            VMEM((2, TILE, NOBS), BF16),
            DMA((6,)),
            DMA((2,)),
        ],
        compiler_params=GRANT,
        cost_estimate=pl.CostEstimate(flops=2 * 15 * NOBS * NOBS * 512, bytes_accessed=32 << 20, transcendentals=0),
    )(order, first, vert, horiz, cell, lev)


def filter_call(where, order, first, vert, horiz, got, pert, mean, taper):
    return pl.pallas_call(
        filter_kernel,
        out_shape=(
            jax.ShapeDtypeStruct((MEMBERS, 1, CELLS), F32),
            jax.ShapeDtypeStruct((1, CELLS), F32),
        ),
        in_specs=[spec(SMEM)] + [spec(HBM)] * 8,
        out_specs=(spec(HBM), spec(VMEM)),
        scratch_shapes=[
            SMEM((8,), jnp.int32),
            SMEM((8, NPATCH), jnp.int32),
            SMEM((NLEV,), F32),
            SMEM((NBIN,), F32),
            VMEM((NPATCH * UNIT, WIDE), BF16),
            VMEM((MEMBERS, CELLS), F32),
            VMEM((1, CELLS), F32),
            VMEM((OWN + CELLS, WIDE), F32),
            VMEM((2, TILE, NOBS), BF16),
            DMA((6,)),
            DMA((PARTS,)),
            DMA((2,)),
        ],
        compiler_params=GRANT,
    )(where, order, first, vert, horiz, got, pert, mean, taper)


def exchange(block, axes):
    return lax.all_to_all(block, axes, 0, 0)


AXES = ("y_hi", "x", "z", "core")


def shards(
    prior_mean,
    prior_pert,
    obs_value,
    obs_var,
    obs_cell,
    obs_level,
    obs_count,
    batch_order,
    horiz_weight,
    vert_weight,
):
    where = jnp.stack([lax.axis_index(AXES), lax.axis_index("y_lo")]).astype(jnp.int32)
    mean = prior_mean
    mine, first = select_call(
        where, batch_order, obs_count, obs_cell, obs_level, obs_value, obs_var, mean, prior_pert
    )
    ring = exchange(mine, ("y_hi", "y_lo")).reshape(2, NLEV, UNIT, WIDE)
    pair = jnp.sum(ring.astype(F32), axis=1).astype(BF16).reshape(1, 2 * UNIT, WIDE)
    group = exchange(jnp.broadcast_to(pair, (4, 2 * UNIT, WIDE)), "x").reshape(8 * UNIT, WIDE)
    group, first = lax.optimization_barrier((group, first))
    got = lax.all_gather(group, ("z", "core"), axis=0, tiled=True)
    taper = taper_call(batch_order, first, vert_weight, horiz_weight, obs_cell, obs_level)
    post_pert, post_mean = filter_call(
        where, batch_order, first, vert_weight, horiz_weight, got, prior_pert, mean, taper
    )
    return post_mean, post_pert


def solution(mesh):
    whole = Mesh(mesh.devices.reshape(2, 4, 8, 2, NLEV), AXES + ("y_lo",))
    return jax.shard_map(
        shards,
        mesh=whole,
        in_specs=(
            P("y_lo", AXES),
            P(None, "y_lo", AXES),
            P(),
            P(),
            P(),
            P(),
            P(),
            P(),
            P(),
            P(),
        ),
        out_specs=(P("y_lo", AXES), P(None, "y_lo", AXES)),
        check_vma=False,
    )
```

```python
import jax
import jax.numpy as jnp
from jax import lax
from jax.experimental import pallas as pl
from jax.experimental.pallas import tpu as pltpu
from jax.sharding import Mesh
from jax.sharding import PartitionSpec as P

MEMBERS = 80
TX = 16
TY = 32
NBATCH = 6
PROWS = 8
NPATCH = 128
NLEV = 4
BIN = 16
NBIN = 16
CAP = 24
NOBS = 1024
CELLS = TX * TY
UNIT = NBATCH * CAP
WIDE = 128
TILE = 1024
PACK = 112
SPAN = 256
LIVE_COLS = NBATCH * NOBS
SLAB = NOBS + 32
OWN = NBATCH * SLAB
PARTS = 4
NTILES = NBATCH * (NBATCH - 1) // 2 * (NOBS // TILE)
INNOV, VAR, POS_X, POS_Y, POS_Z = 80, 83, 86, 87, 88
VMEM = pltpu.VMEM
SMEM = pltpu.SMEM
F32 = jnp.float32
BF16 = jnp.bfloat16


def split3(value):
    high = value.astype(BF16).astype(F32)
    mid = (value - high).astype(BF16).astype(F32)
    return high, mid, value - high - mid


def packed(rows):
    base = jnp.concatenate([rows[:96], rows[120:136]], axis=0)
    thirds = [pltpu.roll(rows[96:120], 96 - 32 * i, 1) for i in range(3)]
    thirds += [pltpu.roll(rows[136:144], 96 - 32 * i, 1) for i in range(3)]
    extra = jnp.concatenate(thirds + [rows[120:136]], axis=0)
    lane = lax.broadcasted_iota(jnp.int32, base.shape, 1)
    return jnp.where(lane < 96, base, extra)


def unpacked(rows):
    def joined(start, size):
        parts = [pltpu.roll(rows[start + i * size : start + (i + 1) * size], 32 * (i + 1), 1) for i in range(3)]
        lane = lax.broadcasted_iota(jnp.int32, parts[0].shape, 1)
        return jnp.where(lane < 32, parts[0], jnp.where(lane < 64, parts[1], parts[2]))

    last = jnp.concatenate([rows[96:112], joined(72, 8)], axis=0)
    return [rows[k * CAP : (k + 1) * CAP] for k in range(4)] + [joined(0, CAP), last]


def fetch(pairs, sems):
    copies = [pltpu.make_async_copy(one, other, sems.at[i]) for i, (one, other) in enumerate(pairs)]
    for copy in copies:
        copy.start()
    for copy in copies:
        copy.wait()


def horizontal(horiz_ref):
    lane = lax.broadcasted_iota(jnp.int32, (1, WIDE), 1)
    table = jnp.zeros((1, WIDE), F32)
    for step in range(NBIN):
        table = jnp.where(lane == step, horiz_ref[step], table)
    return table


def select_kernel(
    where_ref,
    order_hbm,
    count_hbm,
    cell_hbm,
    lev_hbm,
    value_hbm,
    var_hbm,
    mean_hbm,
    pert_hbm,
    out_ref,
    first_ref,
    order_ref,
    count_ref,
    count_all,
    cell_ref,
    lev_ref,
    value_ref,
    var_ref,
    mean_ref,
    pert_ref,
    sems,
):
    patch = where_ref[0]
    level = where_ref[1]
    window = jnp.minimum(patch * CAP // WIDE, NPATCH * CAP // WIDE - 2)
    shift = lax.rem(2 * WIDE - (patch * CAP - window * WIDE), 2 * WIDE)
    start = pl.multiple_of(window * WIDE, WIDE)
    near = pl.ds(start, 2 * WIDE)
    pairs = [
        (order_hbm, order_ref),
        (count_hbm, count_ref),
        (count_hbm, count_all),
        (cell_hbm.at[:, near], cell_ref),
        (lev_hbm.at[:, near], lev_ref),
        (value_hbm.at[:, near], value_ref),
        (var_hbm.at[:, near], var_ref),
        (mean_hbm, mean_ref),
        (pert_hbm.at[:, 0, :], pert_ref),
    ]
    fetch(pairs, sems)

    def column(ref):
        rows = pltpu.roll(ref[...].astype(F32), shift, 1)[:, :WIDE]
        wide = jnp.concatenate([rows, jnp.zeros((WIDE - 8, WIDE), F32)], axis=0).T[:, :8]
        lane = lax.broadcasted_iota(jnp.int32, (CAP, 8), 1)
        wide = wide[:CAP]
        return jnp.concatenate(
            [jnp.sum(jnp.where(lane == order_ref[k], wide, 0.0), axis=1, keepdims=True) for k in range(NBATCH)], axis=0
        )

    one = lax.broadcasted_iota(jnp.int32, (NPATCH, NPATCH), 0)
    other = lax.broadcasted_iota(jnp.int32, (NPATCH, NPATCH), 1)
    before = jnp.where(gathered(one) < gathered(other), 1.0, 0.0).astype(BF16)
    counts = count_all[...].astype(F32).astype(BF16)
    first_ref[...] = jnp.dot(counts, before, preferred_element_type=F32).astype(jnp.int32)

    slot = lax.broadcasted_iota(jnp.int32, (CAP, 1), 0)
    live = jnp.concatenate(
        [(slot < count_ref[order_ref[k], patch]).astype(F32) for k in range(NBATCH)], axis=0
    )
    cell, lev, value, var = column(cell_ref), column(lev_ref), column(value_ref), column(var_ref)
    own = (live > 0.5) & (lev == level.astype(F32))
    mean_parts = split3(mean_ref[...])
    source = jnp.concatenate([pert_ref[...], *mean_parts, jnp.zeros((WIDE - 83, CELLS), F32)], axis=0).astype(BF16)
    spot = lax.broadcasted_iota(jnp.int32, (UNIT, CELLS), 1)
    hot = jnp.where((spot == cell.astype(jnp.int32)) & own, 1.0, 0.0).astype(BF16)
    taken = lax.dot_general(hot, source, (((1,), (1,)), ((), ())), preferred_element_type=F32)
    innov = value - (taken[:, 80:81] + taken[:, 81:82] + taken[:, 82:83])
    across = (cell * (1.0 / TY)).astype(jnp.int32).astype(F32)
    obs_x = across + (patch // PROWS * TX).astype(F32)
    obs_y = cell - across * TY + (patch % PROWS * TY).astype(F32)
    lane = lax.broadcasted_iota(jnp.int32, (UNIT, WIDE), 1)
    out = jnp.where(lane < MEMBERS, taken, 0.0)
    for at, item in enumerate([*split3(innov), *split3(var), obs_x, obs_y, lev]):
        out = jnp.where(lane == INNOV + at, item, out)
    out = packed(jnp.where(own, out, 0.0)).astype(BF16)
    for other in range(2 * NLEV):
        out_ref[other] = out


def gathered(patch):
    return (patch & 15) * 8 + ((patch >> 4) & 3) * 2 + (patch >> 6)


GROUP = [(i >> 1) * 16 + (i & 1) * 64 for i in range(8)]


def first_tile(k):
    return (k + 1) * (NOBS // TILE)


def taper_kernel(
    order_hbm,
    first_hbm,
    vert_hbm,
    horiz_hbm,
    cell_hbm,
    lev_hbm,
    out_hbm,
    order_ref,
    first_ref,
    vert_ref,
    horiz_ref,
    cell_ref,
    lev_ref,
    code_ref,
    slots,
    place,
    hot_x,
    hot_y,
    dist,
    tab_x,
    tab_y,
    levw,
    bufs,
    fetched,
    sems,
):
    fetch(
        [
            (order_hbm, order_ref),
            (first_hbm, first_ref),
            (vert_hbm, vert_ref),
            (horiz_hbm, horiz_ref),
            (cell_hbm, cell_ref),
            (lev_hbm, lev_ref),
        ],
        fetched,
    )
    spot = lax.broadcasted_iota(jnp.int32, (8, NPATCH * CAP), 1).astype(F32)
    patch = ((spot + 0.5) * (1.0 / CAP)).astype(jnp.int32)
    cell = cell_ref[...]
    at_x = (patch // PROWS) * TX + cell // TY
    at_y = (patch % PROWS) * TY + cell % TY
    code_ref[...] = (at_x * 1024 + at_y * NLEV + lev_ref[...]).astype(F32)

    for c in range(NPATCH * CAP // WIDE):
        part = slice(c * WIDE, (c + 1) * WIDE)
        slots[part, :] = jnp.concatenate([code_ref[:, part], jnp.zeros((WIDE - 8, WIDE), F32)], axis=0).T

    def compact(k, unused):
        pick = order_ref[k]

        def put(g, unused):
            for step in GROUP:
                p = g + step
                rows = slots[pl.ds(pl.multiple_of(p * CAP, 8), CAP), :]
                place[pl.ds(k * NOBS + first_ref[pick, p], CAP), :] = rows
            return unused

        return lax.fori_loop(0, NPATCH // 8, put, unused)

    lax.fori_loop(0, NBATCH, compact, 0)

    def mark(t, unused):
        here = pl.ds(pl.multiple_of(t * TILE, TILE), TILE)
        rows = place[here, :]
        lane = lax.broadcasted_iota(jnp.int32, (TILE, WIDE), 1)
        code = jnp.sum(jnp.where(lane == order_ref[t], rows, 0.0), axis=1, keepdims=True)
        code = jnp.broadcast_to(code, (TILE, WIDE))
        place[here, :] = code
        codes = code.astype(jnp.int32)
        hot_x[here, :] = hot(codes >> 10, TILE)
        hot_y[here, :] = hot((codes >> 2) & 255, TILE)
        return unused

    def lookup(bins):
        table = jnp.broadcast_to(horizontal(horiz_ref), (bins.shape[0], WIDE))
        parts = [
            jnp.take_along_axis(table, bins[:, j : j + WIDE], axis=1) for j in range(0, bins.shape[1], WIDE)
        ]
        return jnp.concatenate(parts, axis=1)

    one = lax.broadcasted_iota(jnp.int32, (SPAN, SPAN), 0)
    other = lax.broadcasted_iota(jnp.int32, (SPAN, SPAN), 1)
    apart = jnp.abs(one - other)
    for at, bins in enumerate((jnp.minimum(apart, SPAN - apart) // BIN, apart // BIN)):
        value = lookup(bins)
        high = value.astype(BF16)
        dist[2 * at] = high
        dist[2 * at + 1] = (value - high.astype(F32)).astype(BF16)

    def hot(index, rows):
        lane = lax.broadcasted_iota(jnp.int32, (rows, WIDE), 1)
        parts = [jnp.where(index - j == lane, 1.0, 0.0).astype(BF16) for j in range(0, SPAN, WIDE)]
        return jnp.concatenate(parts, axis=1)

    lax.fori_loop(0, LIVE_COLS // TILE, mark, 0)

    def out_copy(n):
        return pltpu.make_async_copy(bufs.at[n % 2], out_hbm.at[n], sems.at[n % 2])

    def batch(k, n):
        rows = pl.ds(pl.multiple_of(k * NOBS, NOBS), NOBS)
        obs_z = place[rows, :].T[:1].astype(jnp.int32) & 3
        lane = lax.broadcasted_iota(jnp.int32, (1, NOBS), 1)
        vary = 1.0 + (lane & 63).astype(F32) * (1.0 / 64.0)
        contract = (((1,), (1,)), ((), ()))
        for tab, hot_rows, at, factor in ((tab_x, hot_x, 0, vary), (tab_y, hot_y, 2, 1.0 / vary)):
            here = hot_rows[rows, :]
            full = lax.dot_general(dist[at], here, contract, preferred_element_type=F32)
            full = full + lax.dot_general(dist[at + 1], here, contract, preferred_element_type=F32)
            tab[...] = (full * factor).astype(BF16)
        for z in range(NLEV):
            apart = jnp.abs(obs_z - z)
            found = jnp.zeros((1, NOBS), F32)
            for step in range(NLEV):
                found = jnp.where(apart == step, vert_ref[step], found)
            levw[z : z + 1, :] = found

        def tile(t, n):
            here = pl.ds(pl.multiple_of(t * TILE, TILE), TILE)
            lhs_x = hot_x[here, :]
            lhs_y = hot_y[here, :]
            cell_z = place[here, :].astype(jnp.int32) & 3
            cell_z = jnp.concatenate([cell_z, cell_z], axis=1)

            @pl.when(n >= 2)
            def _():
                out_copy(n - 2).wait()

            buf = bufs.at[n % 2]
            for j in range(0, NOBS, SPAN):
                part = slice(j, j + SPAN)
                near = jnp.dot(lhs_x, tab_x[:, part], preferred_element_type=F32)
                far = jnp.dot(lhs_y, tab_y[:, part], preferred_element_type=F32)
                low = jnp.where(cell_z == 0, levw[0:1, part], levw[1:2, part])
                high = jnp.where(cell_z == 2, levw[2:3, part], levw[3:4, part])
                buf[:, part] = (near * far * jnp.where(cell_z < 2, low, high)).astype(BF16)
            out_copy(n).start()
            return n + 1

        return lax.fori_loop(first_tile(k), LIVE_COLS // TILE, tile, n)

    total = lax.fori_loop(0, NBATCH - 1, batch, 0)
    out_copy(total - 2).wait()
    out_copy(total - 1).wait()


def filter_kernel(
    where_ref,
    order_hbm,
    first_hbm,
    vert_hbm,
    horiz_hbm,
    got_hbm,
    pert_hbm,
    mean_hbm,
    taper_hbm,
    post_pert_hbm,
    post_mean_ref,
    order_ref,
    first_ref,
    vert_ref,
    horiz_ref,
    got_ref,
    pert_ref,
    mean_ref,
    state,
    bufs,
    fetched,
    arrived,
    sems,
):
    patch = where_ref[0]
    level = where_ref[1].astype(F32)

    def taper_copy(n):
        return pltpu.make_async_copy(taper_hbm.at[n], bufs.at[n % 2], sems.at[n % 2])

    def part_copy(c):
        rows = pl.ds(c * (NPATCH * PACK // PARTS), NPATCH * PACK // PARTS)
        return pltpu.make_async_copy(got_hbm.at[rows, :], got_ref.at[rows, :], arrived.at[c])

    for c in range(PARTS):
        part_copy(c).start()
    fetch(
        [
            (order_hbm, order_ref),
            (first_hbm, first_ref),
            (vert_hbm, vert_ref),
            (horiz_hbm, horiz_ref),
            (pert_hbm.at[:, 0, :], pert_ref),
            (mean_hbm, mean_ref),
        ],
        fetched,
    )
    taper_copy(0).start()
    own = jnp.concatenate(
        [pert_ref[...], -mean_ref[...], jnp.zeros((WIDE - 81, CELLS), F32)], axis=0
    )
    state[OWN : OWN + CELLS, :] = own.T

    def place(g, unused):
        for i, step in enumerate(GROUP):
            at = pl.multiple_of(g * (8 * PACK) + i * PACK, 16)
            for k, rows in enumerate(unpacked(got_ref[pl.ds(at, PACK), :].astype(F32))):
                first = first_ref[order_ref[k], g + step]
                state[pl.ds(k * SLAB + first, CAP), :] = rows
        return unused

    for c in range(PARTS):
        part_copy(c).wait()
        lax.fori_loop(c * (16 // PARTS), (c + 1) * (16 // PARTS), place, 0)

    def lookup(bins):
        table = jnp.broadcast_to(horizontal(horiz_ref), (bins.shape[0], WIDE))
        parts = [
            jnp.take_along_axis(table, bins[:, j : j + WIDE], axis=1) for j in range(0, bins.shape[1], WIDE)
        ]
        return jnp.concatenate(parts, axis=1)

    def bins_x(one, other):
        apart = jnp.abs(one - other)
        return (jnp.minimum(apart, SPAN - apart) * (1.0 / BIN)).astype(jnp.int32)

    def bins_y(one, other):
        return (jnp.abs(one - other) * (1.0 / BIN)).astype(jnp.int32)

    def vertical(apart):
        found = jnp.zeros_like(apart)
        for step in range(NLEV):
            found = jnp.where(apart == float(step), vert_ref[step], found)
        return found

    def batch(k, n):
        start = pl.multiple_of(k * SLAB, 32)
        block = state[pl.ds(start, NOBS), :].T
        innov = block[INNOV : INNOV + 1] + block[INNOV + 1 : INNOV + 2] + block[INNOV + 2 : INNOV + 3]
        obs_var = block[VAR : VAR + 1] + block[VAR + 1 : VAR + 2] + block[VAR + 2 : VAR + 3]
        obs_x, obs_y, obs_z = block[POS_X : POS_X + 1], block[POS_Y : POS_Y + 1], block[POS_Z : POS_Z + 1]
        row = lax.broadcasted_iota(jnp.int32, (WIDE, NOBS), 0)
        prior = jnp.where(row < MEMBERS, block, 0.0).astype(BF16)
        values = prior.astype(F32)
        spread = jnp.sum(values * values, axis=0, keepdims=True) / (MEMBERS - 1.0) + obs_var
        shrink = 1.0 / (1.0 + jnp.sqrt(obs_var / spread))
        scale = 1.0 / ((MEMBERS - 1.0) * spread)
        coeffs = jnp.where(row == MEMBERS, innov.astype(BF16).astype(F32), values * shrink).T.astype(BF16)

        own_a = lax.broadcasted_iota(jnp.int32, (TX, NOBS), 0) + patch // PROWS * TX
        own_e = lax.broadcasted_iota(jnp.int32, (TY, NOBS), 0) + patch % PROWS * TY
        weight_x = lookup(bins_x(own_a.astype(F32), obs_x)) * (vertical(jnp.abs(obs_z - level)) * scale)
        weight_y = lookup(bins_y(own_e.astype(F32), obs_y))
        cells = state[OWN : OWN + CELLS, :]
        lhs = cells.astype(BF16)
        change = jnp.zeros((CELLS, WIDE), F32)
        for j in range(0, NOBS, SPAN):
            part = slice(j, j + SPAN)
            cov = jnp.dot(lhs, prior[:, part], preferred_element_type=F32)
            gain = jnp.concatenate(
                [
                    (cov[a * TY : (a + 1) * TY] * (weight_x[a : a + 1, part] * weight_y[:, part])).astype(BF16)
                    for a in range(TX)
                ],
                axis=0,
            )
            change = change + jnp.dot(gain, coeffs[part], preferred_element_type=F32)
        state[OWN : OWN + CELLS, :] = cells - change

        def tile(t, n):
            taper_copy(n).wait()

            @pl.when(n < NTILES - 1)
            def _():
                taper_copy(n + 1).start()

            at = pl.multiple_of(t * SLAB, 32)
            cells = state[pl.ds(at, TILE), :]
            lhs = cells.astype(BF16)
            taper = bufs.at[n % 2]
            change = jnp.zeros((TILE, WIDE), F32)
            for j in range(0, NOBS, SPAN):
                part = slice(j, j + SPAN)
                cov = jnp.dot(lhs, prior[:, part], preferred_element_type=F32)
                gain = taper[:, part] * (cov * scale[:, part]).astype(BF16)
                change = change + jnp.dot(gain, coeffs[part], preferred_element_type=F32)
            state[pl.ds(at, TILE), :] = cells - change
            return n + 1

        return lax.fori_loop(first_tile(k), LIVE_COLS // TILE, tile, n)

    lax.fori_loop(0, NBATCH, batch, 0)
    block = state[OWN : OWN + CELLS, :].T
    pert_ref[...] = block[:MEMBERS]
    post_mean_ref[...] = -block[MEMBERS : MEMBERS + 1]
    fetch([(pert_ref, post_pert_hbm.at[:, 0, :])], fetched)


HBM = pltpu.HBM
DMA = pltpu.SemaphoreType.DMA
GRANT = pltpu.CompilerParams(vmem_limit_bytes=60 << 20)


def spec(space):
    return pl.BlockSpec(memory_space=space)


def select_call(where, order, count, cell, lev, value, var, mean, pert):
    return pl.pallas_call(
        select_kernel,
        out_shape=(
            jax.ShapeDtypeStruct((2 * NLEV, PACK, WIDE), BF16),
            jax.ShapeDtypeStruct((8, NPATCH), jnp.int32),
        ),
        in_specs=[spec(SMEM)] + [spec(HBM)] * 8,
        out_specs=(spec(VMEM),) * 2,
        scratch_shapes=[
            SMEM((8,), jnp.int32),
            SMEM((8, NPATCH), jnp.int32),
            VMEM((8, NPATCH), jnp.int32),
            VMEM((8, 2 * WIDE), jnp.int32),
            VMEM((8, 2 * WIDE), jnp.int32),
            VMEM((8, 2 * WIDE), F32),
            VMEM((8, 2 * WIDE), F32),
            VMEM((1, CELLS), F32),
            VMEM((MEMBERS, CELLS), F32),
            DMA((9,)),
        ],
        compiler_params=GRANT,
    )(where, order, count, cell, lev, value, var, mean, pert)


def taper_call(order, first, vert, horiz, cell, lev):
    return pl.pallas_call(
        taper_kernel,
        out_shape=jax.ShapeDtypeStruct((NTILES, TILE, NOBS), BF16),
        in_specs=[spec(HBM)] * 6,
        out_specs=spec(HBM),
        scratch_shapes=[
            SMEM((8,), jnp.int32),
            SMEM((8, NPATCH), jnp.int32),
            SMEM((NLEV,), F32),
            SMEM((NBIN,), F32),
            VMEM((8, NPATCH * CAP), jnp.int32),
            VMEM((8, NPATCH * CAP), jnp.int32),
            VMEM((8, NPATCH * CAP), F32),
            VMEM((NPATCH * CAP, WIDE), F32),
            VMEM((LIVE_COLS + 2 * CAP, WIDE), F32),
            VMEM((LIVE_COLS, SPAN), BF16),
            VMEM((LIVE_COLS, SPAN), BF16),
            VMEM((4, SPAN, SPAN), BF16),
            VMEM((SPAN, NOBS), BF16),
            VMEM((SPAN, NOBS), BF16),
            VMEM((8, NOBS), F32),
            VMEM((2, TILE, NOBS), BF16),
            DMA((6,)),
            DMA((2,)),
        ],
        compiler_params=GRANT,
        cost_estimate=pl.CostEstimate(flops=2 * 15 * NOBS * NOBS * 512, bytes_accessed=32 << 20, transcendentals=0),
    )(order, first, vert, horiz, cell, lev)


def filter_call(where, order, first, vert, horiz, got, pert, mean, taper):
    return pl.pallas_call(
        filter_kernel,
        out_shape=(
            jax.ShapeDtypeStruct((MEMBERS, 1, CELLS), F32),
            jax.ShapeDtypeStruct((1, CELLS), F32),
        ),
        in_specs=[spec(SMEM)] + [spec(HBM)] * 8,
        out_specs=(spec(HBM), spec(VMEM)),
        scratch_shapes=[
            SMEM((8,), jnp.int32),
            SMEM((8, NPATCH), jnp.int32),
            SMEM((NLEV,), F32),
            SMEM((NBIN,), F32),
            VMEM((NPATCH * PACK, WIDE), BF16),
            VMEM((MEMBERS, CELLS), F32),
            VMEM((1, CELLS), F32),
            VMEM((OWN + CELLS, WIDE), F32),
            VMEM((2, TILE, NOBS), BF16),
            DMA((6,)),
            DMA((PARTS,)),
            DMA((2,)),
        ],
        compiler_params=GRANT,
    )(where, order, first, vert, horiz, got, pert, mean, taper)


def exchange(block, axes):
    return lax.all_to_all(block, axes, 0, 0)


AXES = ("y_hi", "x", "z", "core")


def shards(
    prior_mean,
    prior_pert,
    obs_value,
    obs_var,
    obs_cell,
    obs_level,
    obs_count,
    batch_order,
    horiz_weight,
    vert_weight,
):
    where = jnp.stack([lax.axis_index(AXES), lax.axis_index("y_lo")]).astype(jnp.int32)
    mean = prior_mean
    mine, first = select_call(
        where, batch_order, obs_count, obs_cell, obs_level, obs_value, obs_var, mean, prior_pert
    )
    ring = exchange(mine, ("y_hi", "y_lo")).reshape(2, NLEV, PACK, WIDE)
    pair = jnp.sum(ring.astype(F32), axis=1).astype(BF16).reshape(1, 2 * PACK, WIDE)
    group = exchange(jnp.broadcast_to(pair, (4, 2 * PACK, WIDE)), "x").reshape(8 * PACK, WIDE)
    group, first = lax.optimization_barrier((group, first))
    got = lax.all_gather(group, ("z", "core"), axis=0, tiled=True)
    taper = taper_call(batch_order, first, vert_weight, horiz_weight, obs_cell, obs_level)
    post_pert, post_mean = filter_call(
        where, batch_order, first, vert_weight, horiz_weight, got, prior_pert, mean, taper
    )
    return post_mean, post_pert


def solution(mesh):
    whole = Mesh(mesh.devices.reshape(2, 4, 8, 2, NLEV), AXES + ("y_lo",))
    return jax.shard_map(
        shards,
        mesh=whole,
        in_specs=(
            P("y_lo", AXES),
            P(None, "y_lo", AXES),
            P(),
            P(),
            P(),
            P(),
            P(),
            P(),
            P(),
            P(),
        ),
        out_specs=(P("y_lo", AXES), P(None, "y_lo", AXES)),
        check_vma=False,
    )
```

```python
import jax
import jax.numpy as jnp
from jax import lax
from jax.experimental import pallas as pl
from jax.experimental.pallas import tpu as pltpu
from jax.sharding import Mesh
from jax.sharding import PartitionSpec as P

MEMBERS = 80
TX = 16
TY = 32
NBATCH = 6
PROWS = 8
NPATCH = 128
NLEV = 4
BIN = 16
NBIN = 16
CAP = 24
NOBS = 1024
CELLS = TX * TY
UNIT = NBATCH * CAP
WIDE = 128
TILE = 1024
PACK = 112
SPAN = 256
LIVE_COLS = NBATCH * NOBS
SLAB = NOBS + 32
OWN = NBATCH * SLAB
PARTS = 4
NTILES = NBATCH * (NBATCH - 1) // 2 * (NOBS // TILE)
INNOV, VAR, POS_X, POS_Y, POS_Z = 80, 83, 86, 87, 88
VMEM = pltpu.VMEM
SMEM = pltpu.SMEM
F32 = jnp.float32
BF16 = jnp.bfloat16


def split3(value):
    high = value.astype(BF16).astype(F32)
    mid = (value - high).astype(BF16).astype(F32)
    return high, mid, value - high - mid


def packed(rows):
    base = jnp.concatenate([rows[:96], rows[120:136]], axis=0)
    thirds = [pltpu.roll(rows[96:120], 96 - 32 * i, 1) for i in range(3)]
    thirds += [pltpu.roll(rows[136:144], 96 - 32 * i, 1) for i in range(3)]
    extra = jnp.concatenate(thirds + [rows[120:136]], axis=0)
    lane = lax.broadcasted_iota(jnp.int32, base.shape, 1)
    return jnp.where(lane < 96, base, extra)


def unpacked(rows):
    def joined(start, size):
        parts = [pltpu.roll(rows[start + i * size : start + (i + 1) * size], 32 * (i + 1), 1) for i in range(3)]
        lane = lax.broadcasted_iota(jnp.int32, parts[0].shape, 1)
        return jnp.where(lane < 32, parts[0], jnp.where(lane < 64, parts[1], parts[2]))

    last = jnp.concatenate([rows[96:112], joined(72, 8)], axis=0)
    return [rows[k * CAP : (k + 1) * CAP] for k in range(4)] + [joined(0, CAP), last]


def fetch(pairs, sems):
    copies = [pltpu.make_async_copy(one, other, sems.at[i]) for i, (one, other) in enumerate(pairs)]
    for copy in copies:
        copy.start()
    for copy in copies:
        copy.wait()


def horizontal(horiz_ref):
    lane = lax.broadcasted_iota(jnp.int32, (1, WIDE), 1)
    table = jnp.zeros((1, WIDE), F32)
    for step in range(NBIN):
        table = jnp.where(lane == step, horiz_ref[step], table)
    return table


def select_kernel(
    where_ref,
    order_hbm,
    count_hbm,
    cell_hbm,
    lev_hbm,
    value_hbm,
    var_hbm,
    mean_hbm,
    pert_hbm,
    out_ref,
    first_ref,
    order_ref,
    count_ref,
    count_all,
    cell_ref,
    lev_ref,
    value_ref,
    var_ref,
    mean_ref,
    pert_ref,
    sems,
):
    patch = where_ref[0]
    level = where_ref[1]
    window = jnp.minimum(patch * CAP // WIDE, NPATCH * CAP // WIDE - 2)
    shift = lax.rem(2 * WIDE - (patch * CAP - window * WIDE), 2 * WIDE)
    start = pl.multiple_of(window * WIDE, WIDE)
    near = pl.ds(start, 2 * WIDE)
    pairs = [
        (order_hbm, order_ref),
        (count_hbm, count_ref),
        (count_hbm, count_all),
        (cell_hbm.at[:, near], cell_ref),
        (lev_hbm.at[:, near], lev_ref),
        (value_hbm.at[:, near], value_ref),
        (var_hbm.at[:, near], var_ref),
        (mean_hbm, mean_ref),
        (pert_hbm.at[:, 0, :], pert_ref),
    ]
    fetch(pairs, sems)

    def column(ref):
        rows = pltpu.roll(ref[...].astype(F32), shift, 1)[:, :WIDE]
        wide = jnp.concatenate([rows, jnp.zeros((WIDE - 8, WIDE), F32)], axis=0).T[:, :8]
        lane = lax.broadcasted_iota(jnp.int32, (CAP, 8), 1)
        wide = wide[:CAP]
        return jnp.concatenate(
            [jnp.sum(jnp.where(lane == order_ref[k], wide, 0.0), axis=1, keepdims=True) for k in range(NBATCH)], axis=0
        )

    one = lax.broadcasted_iota(jnp.int32, (NPATCH, NPATCH), 0)
    other = lax.broadcasted_iota(jnp.int32, (NPATCH, NPATCH), 1)
    before = jnp.where(gathered(one) < gathered(other), 1.0, 0.0).astype(BF16)
    counts = count_all[...].astype(F32).astype(BF16)
    first_ref[...] = jnp.dot(counts, before, preferred_element_type=F32).astype(jnp.int32)

    slot = lax.broadcasted_iota(jnp.int32, (CAP, 1), 0)
    live = jnp.concatenate(
        [(slot < count_ref[order_ref[k], patch]).astype(F32) for k in range(NBATCH)], axis=0
    )
    cell, lev, value, var = column(cell_ref), column(lev_ref), column(value_ref), column(var_ref)
    own = (live > 0.5) & (lev == level.astype(F32))
    mean_parts = split3(mean_ref[...])
    source = jnp.concatenate([pert_ref[...], *mean_parts, jnp.zeros((WIDE - 83, CELLS), F32)], axis=0).astype(BF16)
    spot = lax.broadcasted_iota(jnp.int32, (UNIT, CELLS), 1)
    hot = jnp.where((spot == cell.astype(jnp.int32)) & own, 1.0, 0.0).astype(BF16)
    taken = lax.dot_general(hot, source, (((1,), (1,)), ((), ())), preferred_element_type=F32)
    innov = value - (taken[:, 80:81] + taken[:, 81:82] + taken[:, 82:83])
    across = (cell * (1.0 / TY)).astype(jnp.int32).astype(F32)
    obs_x = across + (patch // PROWS * TX).astype(F32)
    obs_y = cell - across * TY + (patch % PROWS * TY).astype(F32)
    lane = lax.broadcasted_iota(jnp.int32, (UNIT, WIDE), 1)
    out = jnp.where(lane < MEMBERS, taken, 0.0)
    for at, item in enumerate([*split3(innov), *split3(var), obs_x, obs_y, lev]):
        out = jnp.where(lane == INNOV + at, item, out)
    out = packed(jnp.where(own, out, 0.0)).astype(BF16)
    for other in range(2 * NLEV):
        out_ref[other] = out


def gathered(patch):
    return (patch & 15) * 8 + ((patch >> 4) & 3) * 2 + (patch >> 6)


GROUP = [(i >> 1) * 16 + (i & 1) * 64 for i in range(8)]


def first_tile(k):
    return (k + 1) * (NOBS // TILE)


def taper_kernel(
    order_hbm,
    first_hbm,
    vert_hbm,
    horiz_hbm,
    cell_hbm,
    lev_hbm,
    out_hbm,
    order_ref,
    first_ref,
    vert_ref,
    horiz_ref,
    cell_ref,
    lev_ref,
    code_ref,
    slots,
    place,
    hot_x,
    hot_y,
    dist,
    tab_x,
    tab_y,
    levw,
    bufs,
    fetched,
    sems,
):
    fetch(
        [
            (order_hbm, order_ref),
            (first_hbm, first_ref),
            (vert_hbm, vert_ref),
            (horiz_hbm, horiz_ref),
            (cell_hbm, cell_ref),
            (lev_hbm, lev_ref),
        ],
        fetched,
    )
    spot = lax.broadcasted_iota(jnp.int32, (8, NPATCH * CAP), 1).astype(F32)
    patch = ((spot + 0.5) * (1.0 / CAP)).astype(jnp.int32)
    cell = cell_ref[...]
    at_x = (patch // PROWS) * TX + cell // TY
    at_y = (patch % PROWS) * TY + cell % TY
    code_ref[...] = (at_x * 1024 + at_y * NLEV + lev_ref[...]).astype(F32)

    for c in range(NPATCH * CAP // WIDE):
        part = slice(c * WIDE, (c + 1) * WIDE)
        slots[part, :] = jnp.concatenate([code_ref[:, part], jnp.zeros((WIDE - 8, WIDE), F32)], axis=0).T

    def compact(k, unused):
        pick = order_ref[k]

        def put(g, unused):
            for step in GROUP:
                p = g + step
                rows = slots[pl.ds(pl.multiple_of(p * CAP, 8), CAP), :]
                place[pl.ds(k * NOBS + first_ref[pick, p], CAP), :] = rows
            return unused

        return lax.fori_loop(0, NPATCH // 8, put, unused)

    lax.fori_loop(0, NBATCH, compact, 0)

    def mark(t, unused):
        here = pl.ds(pl.multiple_of(t * TILE, TILE), TILE)
        rows = place[here, :]
        lane = lax.broadcasted_iota(jnp.int32, (TILE, WIDE), 1)
        code = jnp.sum(jnp.where(lane == order_ref[t], rows, 0.0), axis=1, keepdims=True)
        code = jnp.broadcast_to(code, (TILE, WIDE))
        place[here, :] = code
        codes = code.astype(jnp.int32)
        hot_x[here, :] = hot(codes >> 10, TILE)
        hot_y[here, :] = hot((codes >> 2) & 255, TILE)
        return unused

    def lookup(bins):
        table = jnp.broadcast_to(horizontal(horiz_ref), (bins.shape[0], WIDE))
        parts = [
            jnp.take_along_axis(table, bins[:, j : j + WIDE], axis=1) for j in range(0, bins.shape[1], WIDE)
        ]
        return jnp.concatenate(parts, axis=1)

    one = lax.broadcasted_iota(jnp.int32, (SPAN, SPAN), 0)
    other = lax.broadcasted_iota(jnp.int32, (SPAN, SPAN), 1)
    apart = jnp.abs(one - other)
    for at, bins in enumerate((jnp.minimum(apart, SPAN - apart) // BIN, apart // BIN)):
        value = lookup(bins)
        high = value.astype(BF16)
        dist[2 * at] = high
        dist[2 * at + 1] = (value - high.astype(F32)).astype(BF16)

    def hot(index, rows):
        lane = lax.broadcasted_iota(jnp.int32, (rows, WIDE), 1)
        parts = [jnp.where(index - j == lane, 1.0, 0.0).astype(BF16) for j in range(0, SPAN, WIDE)]
        return jnp.concatenate(parts, axis=1)

    lax.fori_loop(0, LIVE_COLS // TILE, mark, 0)

    def out_copy(n):
        return pltpu.make_async_copy(bufs.at[n % 2], out_hbm.at[n], sems.at[n % 2])

    def batch(k, n):
        rows = pl.ds(pl.multiple_of(k * NOBS, NOBS), NOBS)
        obs_z = place[rows, :].T[:1].astype(jnp.int32) & 3
        lane = lax.broadcasted_iota(jnp.int32, (1, NOBS), 1)
        vary = 1.0 + (lane & 63).astype(F32) * (1.0 / 64.0)
        contract = (((1,), (1,)), ((), ()))
        for tab, hot_rows, at, factor in ((tab_x, hot_x, 0, vary), (tab_y, hot_y, 2, 1.0 / vary)):
            here = hot_rows[rows, :]
            full = lax.dot_general(dist[at], here, contract, preferred_element_type=F32)
            full = full + lax.dot_general(dist[at + 1], here, contract, preferred_element_type=F32)
            tab[...] = (full * factor).astype(BF16)
        for z in range(NLEV):
            apart = jnp.abs(obs_z - z)
            found = jnp.zeros((1, NOBS), F32)
            for step in range(NLEV):
                found = jnp.where(apart == step, vert_ref[step], found)
            levw[z : z + 1, :] = found

        def tile(t, n):
            here = pl.ds(pl.multiple_of(t * TILE, TILE), TILE)
            lhs_x = hot_x[here, :]
            lhs_y = hot_y[here, :]
            cell_z = place[here, :].astype(jnp.int32) & 3
            cell_z = jnp.concatenate([cell_z, cell_z], axis=1)

            @pl.when(n >= 2)
            def _():
                out_copy(n - 2).wait()

            buf = bufs.at[n % 2]
            for j in range(0, NOBS, SPAN):
                part = slice(j, j + SPAN)
                near = jnp.dot(lhs_x, tab_x[:, part], preferred_element_type=F32)
                far = jnp.dot(lhs_y, tab_y[:, part], preferred_element_type=F32)
                low = jnp.where(cell_z == 0, levw[0:1, part], levw[1:2, part])
                high = jnp.where(cell_z == 2, levw[2:3, part], levw[3:4, part])
                buf[:, part] = (near * far * jnp.where(cell_z < 2, low, high)).astype(BF16)
            out_copy(n).start()
            return n + 1

        return lax.fori_loop(first_tile(k), LIVE_COLS // TILE, tile, n)

    total = lax.fori_loop(0, NBATCH - 1, batch, 0)
    out_copy(total - 2).wait()
    out_copy(total - 1).wait()


def filter_kernel(
    where_ref,
    order_hbm,
    first_hbm,
    vert_hbm,
    horiz_hbm,
    got_hbm,
    pert_hbm,
    mean_hbm,
    taper_hbm,
    post_pert_hbm,
    post_mean_ref,
    order_ref,
    first_ref,
    vert_ref,
    horiz_ref,
    got_ref,
    pert_ref,
    mean_ref,
    state,
    prior,
    coeffs,
    lines,
    bufs,
    fetched,
    arrived,
    sems,
):
    patch = where_ref[0]
    level = where_ref[1].astype(F32)

    def taper_copy(n):
        return pltpu.make_async_copy(taper_hbm.at[n], bufs.at[n % 2], sems.at[n % 2])

    def part_copy(c):
        rows = pl.ds(c * (NPATCH * PACK // PARTS), NPATCH * PACK // PARTS)
        return pltpu.make_async_copy(got_hbm.at[rows, :], got_ref.at[rows, :], arrived.at[c])

    for c in range(PARTS):
        part_copy(c).start()
    fetch(
        [
            (order_hbm, order_ref),
            (first_hbm, first_ref),
            (vert_hbm, vert_ref),
            (horiz_hbm, horiz_ref),
            (pert_hbm.at[:, 0, :], pert_ref),
            (mean_hbm, mean_ref),
        ],
        fetched,
    )
    taper_copy(0).start()
    own = jnp.concatenate(
        [pert_ref[...], -mean_ref[...], jnp.zeros((WIDE - 81, CELLS), F32)], axis=0
    )
    state[OWN : OWN + CELLS, :] = own.T

    def place(g, unused):
        for i, step in enumerate(GROUP):
            at = pl.multiple_of(g * (8 * PACK) + i * PACK, 16)
            for k, rows in enumerate(unpacked(got_ref[pl.ds(at, PACK), :].astype(F32))):
                first = first_ref[order_ref[k], g + step]
                state[pl.ds(k * SLAB + first, CAP), :] = rows
        return unused

    for c in range(PARTS):
        part_copy(c).wait()
        lax.fori_loop(c * (16 // PARTS), (c + 1) * (16 // PARTS), place, 0)

    def lookup(bins):
        table = jnp.broadcast_to(horizontal(horiz_ref), (bins.shape[0], WIDE))
        parts = [
            jnp.take_along_axis(table, bins[:, j : j + WIDE], axis=1) for j in range(0, bins.shape[1], WIDE)
        ]
        return jnp.concatenate(parts, axis=1)

    def bins_x(one, other):
        apart = jnp.abs(one - other)
        return (jnp.minimum(apart, SPAN - apart) * (1.0 / BIN)).astype(jnp.int32)

    def bins_y(one, other):
        return (jnp.abs(one - other) * (1.0 / BIN)).astype(jnp.int32)

    def vertical(apart):
        found = jnp.zeros_like(apart)
        for step in range(NLEV):
            found = jnp.where(apart == float(step), vert_ref[step], found)
        return found

    def slab(k):
        return pl.ds(pl.multiple_of(k * SLAB, 32), NOBS)

    def prepare(k, slot):
        block = state[slab(k), :].T
        innov = block[INNOV : INNOV + 1] + block[INNOV + 1 : INNOV + 2] + block[INNOV + 2 : INNOV + 3]
        obs_var = block[VAR : VAR + 1] + block[VAR + 1 : VAR + 2] + block[VAR + 2 : VAR + 3]
        row = lax.broadcasted_iota(jnp.int32, (WIDE, NOBS), 0)
        rounded = jnp.where(row < MEMBERS, block, 0.0).astype(BF16)
        values = rounded.astype(F32)
        spread = jnp.sum(values * values, axis=0, keepdims=True) / (MEMBERS - 1.0) + obs_var
        shrink = 1.0 / (1.0 + jnp.sqrt(obs_var / spread))
        prior[slot] = rounded
        lines[slot, 0:1] = 1.0 / ((MEMBERS - 1.0) * spread)
        lines[slot, 1:4] = block[POS_X : POS_Z + 1]
        coeffs[slot] = jnp.where(row == MEMBERS, innov.astype(BF16).astype(F32), values * shrink).T.astype(BF16)

    def own_update(slot, cells):
        scale, obs_x = lines[slot, 0:1], lines[slot, 1:2]
        obs_y, obs_z = lines[slot, 2:3], lines[slot, 3:4]
        own_a = lax.broadcasted_iota(jnp.int32, (TX, NOBS), 0) + patch // PROWS * TX
        own_e = lax.broadcasted_iota(jnp.int32, (TY, NOBS), 0) + patch % PROWS * TY
        weight_x = lookup(bins_x(own_a.astype(F32), obs_x)) * (vertical(jnp.abs(obs_z - level)) * scale)
        weight_y = lookup(bins_y(own_e.astype(F32), obs_y))
        lhs = cells.astype(BF16)
        change = jnp.zeros((CELLS, WIDE), F32)
        for j in range(0, NOBS, SPAN):
            part = slice(j, j + SPAN)
            cov = jnp.dot(lhs, prior[slot, :, part], preferred_element_type=F32)
            gain = jnp.concatenate(
                [
                    (cov[a * TY : (a + 1) * TY] * (weight_x[a : a + 1, part] * weight_y[:, part])).astype(BF16)
                    for a in range(TX)
                ],
                axis=0,
            )
            change = change + jnp.dot(gain, coeffs[slot, part], preferred_element_type=F32)
        return cells - change

    def pair_update(slot, cells, n):
        scale = lines[slot, 0:1]
        lhs = cells.astype(BF16)
        taper = bufs.at[n % 2]
        change = jnp.zeros((TILE, WIDE), F32)
        for j in range(0, NOBS, SPAN):
            part = slice(j, j + SPAN)
            cov = jnp.dot(lhs, prior[slot, :, part], preferred_element_type=F32)
            gain = taper[:, part] * (cov * scale[:, part]).astype(BF16)
            change = change + jnp.dot(gain, coeffs[slot, part], preferred_element_type=F32)
        return cells - change

    def next_taper(n):
        taper_copy(n).wait()

        @pl.when(n < NTILES - 1)
        def _():
            taper_copy(n + 1).start()

    def own_and_first(k, slot, n):
        next_taper(n)
        mine, first = state[OWN : OWN + CELLS, :], state[slab(k + 1), :]
        mine, first = own_update(slot, mine), pair_update(slot, first, n)
        state[OWN : OWN + CELLS, :] = mine
        state[slab(k + 1), :] = first

    def batch(k, slot, n):
        own_and_first(k, slot, n)
        next_taper(n + 1)
        cells = state[slab(k + 2), :]
        prepare(k + 1, 1 - slot)
        state[slab(k + 2), :] = pair_update(slot, cells, n + 1)

        def tile(t, n):
            next_taper(n)
            state[slab(t), :] = pair_update(slot, state[slab(t), :], n)
            return n + 1

        return lax.fori_loop(k + 3, NBATCH, tile, n + 2)

    def two(i, n):
        return batch(2 * i + 1, 1, batch(2 * i, 0, n))

    prepare(0, 0)
    total = lax.fori_loop(0, NBATCH // 2 - 1, two, 0)
    own_and_first(NBATCH - 2, 0, total)
    prepare(NBATCH - 1, 1)
    state[OWN : OWN + CELLS, :] = own_update(1, state[OWN : OWN + CELLS, :])
    block = state[OWN : OWN + CELLS, :].T
    pert_ref[...] = block[:MEMBERS]
    post_mean_ref[...] = -block[MEMBERS : MEMBERS + 1]
    fetch([(pert_ref, post_pert_hbm.at[:, 0, :])], fetched)


HBM = pltpu.HBM
DMA = pltpu.SemaphoreType.DMA
GRANT = pltpu.CompilerParams(vmem_limit_bytes=60 << 20)


def spec(space):
    return pl.BlockSpec(memory_space=space)


def select_call(where, order, count, cell, lev, value, var, mean, pert):
    return pl.pallas_call(
        select_kernel,
        out_shape=(
            jax.ShapeDtypeStruct((2 * NLEV, PACK, WIDE), BF16),
            jax.ShapeDtypeStruct((8, NPATCH), jnp.int32),
        ),
        in_specs=[spec(SMEM)] + [spec(HBM)] * 8,
        out_specs=(spec(VMEM),) * 2,
        scratch_shapes=[
            SMEM((8,), jnp.int32),
            SMEM((8, NPATCH), jnp.int32),
            VMEM((8, NPATCH), jnp.int32),
            VMEM((8, 2 * WIDE), jnp.int32),
            VMEM((8, 2 * WIDE), jnp.int32),
            VMEM((8, 2 * WIDE), F32),
            VMEM((8, 2 * WIDE), F32),
            VMEM((1, CELLS), F32),
            VMEM((MEMBERS, CELLS), F32),
            DMA((9,)),
        ],
        compiler_params=GRANT,
    )(where, order, count, cell, lev, value, var, mean, pert)


def taper_call(order, first, vert, horiz, cell, lev):
    return pl.pallas_call(
        taper_kernel,
        out_shape=jax.ShapeDtypeStruct((NTILES, TILE, NOBS), BF16),
        in_specs=[spec(HBM)] * 6,
        out_specs=spec(HBM),
        scratch_shapes=[
            SMEM((8,), jnp.int32),
            SMEM((8, NPATCH), jnp.int32),
            SMEM((NLEV,), F32),
            SMEM((NBIN,), F32),
            VMEM((8, NPATCH * CAP), jnp.int32),
            VMEM((8, NPATCH * CAP), jnp.int32),
            VMEM((8, NPATCH * CAP), F32),
            VMEM((NPATCH * CAP, WIDE), F32),
            VMEM((LIVE_COLS + 2 * CAP, WIDE), F32),
            VMEM((LIVE_COLS, SPAN), BF16),
            VMEM((LIVE_COLS, SPAN), BF16),
            VMEM((4, SPAN, SPAN), BF16),
            VMEM((SPAN, NOBS), BF16),
            VMEM((SPAN, NOBS), BF16),
            VMEM((8, NOBS), F32),
            VMEM((2, TILE, NOBS), BF16),
            DMA((6,)),
            DMA((2,)),
        ],
        compiler_params=GRANT,
        cost_estimate=pl.CostEstimate(flops=2 * 15 * NOBS * NOBS * 512, bytes_accessed=32 << 20, transcendentals=0),
    )(order, first, vert, horiz, cell, lev)


def filter_call(where, order, first, vert, horiz, got, pert, mean, taper):
    return pl.pallas_call(
        filter_kernel,
        out_shape=(
            jax.ShapeDtypeStruct((MEMBERS, 1, CELLS), F32),
            jax.ShapeDtypeStruct((1, CELLS), F32),
        ),
        in_specs=[spec(SMEM)] + [spec(HBM)] * 8,
        out_specs=(spec(HBM), spec(VMEM)),
        scratch_shapes=[
            SMEM((8,), jnp.int32),
            SMEM((8, NPATCH), jnp.int32),
            SMEM((NLEV,), F32),
            SMEM((NBIN,), F32),
            VMEM((NPATCH * PACK, WIDE), BF16),
            VMEM((MEMBERS, CELLS), F32),
            VMEM((1, CELLS), F32),
            VMEM((OWN + CELLS, WIDE), F32),
            VMEM((2, WIDE, NOBS), BF16),
            VMEM((2, NOBS, WIDE), BF16),
            VMEM((2, 8, NOBS), F32),
            VMEM((2, TILE, NOBS), BF16),
            DMA((6,)),
            DMA((PARTS,)),
            DMA((2,)),
        ],
        compiler_params=GRANT,
    )(where, order, first, vert, horiz, got, pert, mean, taper)


def exchange(block, axes):
    return lax.all_to_all(block, axes, 0, 0)


AXES = ("y_hi", "x", "z", "core")


def shards(
    prior_mean,
    prior_pert,
    obs_value,
    obs_var,
    obs_cell,
    obs_level,
    obs_count,
    batch_order,
    horiz_weight,
    vert_weight,
):
    where = jnp.stack([lax.axis_index(AXES), lax.axis_index("y_lo")]).astype(jnp.int32)
    mean = prior_mean
    mine, first = select_call(
        where, batch_order, obs_count, obs_cell, obs_level, obs_value, obs_var, mean, prior_pert
    )
    ring = exchange(mine, ("y_hi", "y_lo")).reshape(2, NLEV, PACK, WIDE)
    pair = jnp.sum(ring.astype(F32), axis=1).astype(BF16).reshape(1, 2 * PACK, WIDE)
    group = exchange(jnp.broadcast_to(pair, (4, 2 * PACK, WIDE)), "x").reshape(8 * PACK, WIDE)
    group, first = lax.optimization_barrier((group, first))
    got = lax.all_gather(group, ("z", "core"), axis=0, tiled=True)
    taper = taper_call(batch_order, first, vert_weight, horiz_weight, obs_cell, obs_level)
    post_pert, post_mean = filter_call(
        where, batch_order, first, vert_weight, horiz_weight, got, prior_pert, mean, taper
    )
    return post_mean, post_pert


def solution(mesh):
    whole = Mesh(mesh.devices.reshape(2, 4, 8, 2, NLEV), AXES + ("y_lo",))
    return jax.shard_map(
        shards,
        mesh=whole,
        in_specs=(
            P("y_lo", AXES),
            P(None, "y_lo", AXES),
            P(),
            P(),
            P(),
            P(),
            P(),
            P(),
            P(),
            P(),
        ),
        out_specs=(P("y_lo", AXES), P(None, "y_lo", AXES)),
        check_vma=False,
    )
```

```python
import jax
import jax.numpy as jnp
from jax import lax
from jax.experimental import pallas as pl
from jax.experimental.pallas import tpu as pltpu
from jax.sharding import Mesh
from jax.sharding import PartitionSpec as P

MEMBERS = 80
TX = 16
TY = 32
NBATCH = 6
PROWS = 8
NPATCH = 128
NLEV = 4
BIN = 16
NBIN = 16
CAP = 24
NOBS = 1024
CELLS = TX * TY
UNIT = NBATCH * CAP
WIDE = 128
TILE = 1024
PACK = 112
SPAN = 256
LIVE_COLS = NBATCH * NOBS
SLAB = NOBS + 32
OWN = NBATCH * SLAB
PARTS = 4
NTILES = NBATCH * (NBATCH - 1) // 2 * (NOBS // TILE)
INNOV, VAR, POS_X, POS_Y, POS_Z = 80, 83, 86, 87, 88
VMEM = pltpu.VMEM
SMEM = pltpu.SMEM
F32 = jnp.float32
BF16 = jnp.bfloat16


def split3(value):
    high = value.astype(BF16).astype(F32)
    mid = (value - high).astype(BF16).astype(F32)
    return high, mid, value - high - mid


def packed(rows):
    base = jnp.concatenate([rows[:96], rows[120:136]], axis=0)
    thirds = [pltpu.roll(rows[96:120], 96 - 32 * i, 1) for i in range(3)]
    thirds += [pltpu.roll(rows[136:144], 96 - 32 * i, 1) for i in range(3)]
    extra = jnp.concatenate(thirds + [rows[120:136]], axis=0)
    lane = lax.broadcasted_iota(jnp.int32, base.shape, 1)
    return jnp.where(lane < 96, base, extra)


def unpacked(rows):
    def joined(start, size):
        parts = [pltpu.roll(rows[start + i * size : start + (i + 1) * size], 32 * (i + 1), 1) for i in range(3)]
        lane = lax.broadcasted_iota(jnp.int32, parts[0].shape, 1)
        return jnp.where(lane < 32, parts[0], jnp.where(lane < 64, parts[1], parts[2]))

    last = jnp.concatenate([rows[96:112], joined(72, 8)], axis=0)
    return [rows[k * CAP : (k + 1) * CAP] for k in range(4)] + [joined(0, CAP), last]


def fetch(pairs, sems):
    copies = [pltpu.make_async_copy(one, other, sems.at[i]) for i, (one, other) in enumerate(pairs)]
    for copy in copies:
        copy.start()
    for copy in copies:
        copy.wait()


def horizontal(horiz_ref):
    lane = lax.broadcasted_iota(jnp.int32, (1, WIDE), 1)
    table = jnp.zeros((1, WIDE), F32)
    for step in range(NBIN):
        table = jnp.where(lane == step, horiz_ref[step], table)
    return table


def select_kernel(
    where_ref,
    order_hbm,
    count_hbm,
    cell_hbm,
    lev_hbm,
    value_hbm,
    var_hbm,
    mean_hbm,
    pert_hbm,
    out_ref,
    first_ref,
    order_ref,
    count_ref,
    count_all,
    cell_ref,
    lev_ref,
    value_ref,
    var_ref,
    mean_ref,
    pert_ref,
    sems,
):
    patch = where_ref[0]
    level = where_ref[1]
    window = jnp.minimum(patch * CAP // WIDE, NPATCH * CAP // WIDE - 2)
    shift = lax.rem(2 * WIDE - (patch * CAP - window * WIDE), 2 * WIDE)
    start = pl.multiple_of(window * WIDE, WIDE)
    near = pl.ds(start, 2 * WIDE)
    pairs = [
        (order_hbm, order_ref),
        (count_hbm, count_ref),
        (count_hbm, count_all),
        (cell_hbm.at[:, near], cell_ref),
        (lev_hbm.at[:, near], lev_ref),
        (value_hbm.at[:, near], value_ref),
        (var_hbm.at[:, near], var_ref),
        (mean_hbm, mean_ref),
        (pert_hbm.at[:, 0, :], pert_ref),
    ]
    fetch(pairs, sems)

    def column(ref):
        rows = pltpu.roll(ref[...].astype(F32), shift, 1)[:, :WIDE]
        wide = jnp.concatenate([rows, jnp.zeros((WIDE - 8, WIDE), F32)], axis=0).T[:, :8]
        lane = lax.broadcasted_iota(jnp.int32, (CAP, 8), 1)
        wide = wide[:CAP]
        return jnp.concatenate(
            [jnp.sum(jnp.where(lane == order_ref[k], wide, 0.0), axis=1, keepdims=True) for k in range(NBATCH)], axis=0
        )

    one = lax.broadcasted_iota(jnp.int32, (NPATCH, NPATCH), 0)
    other = lax.broadcasted_iota(jnp.int32, (NPATCH, NPATCH), 1)
    before = jnp.where(gathered(one) < gathered(other), 1.0, 0.0).astype(BF16)
    counts = count_all[...].astype(F32).astype(BF16)
    first_ref[...] = jnp.dot(counts, before, preferred_element_type=F32).astype(jnp.int32)

    slot = lax.broadcasted_iota(jnp.int32, (CAP, 1), 0)
    live = jnp.concatenate(
        [(slot < count_ref[order_ref[k], patch]).astype(F32) for k in range(NBATCH)], axis=0
    )
    cell, lev, value, var = column(cell_ref), column(lev_ref), column(value_ref), column(var_ref)
    own = (live > 0.5) & (lev == level.astype(F32))
    mean_parts = split3(mean_ref[...])
    source = jnp.concatenate([pert_ref[...], *mean_parts, jnp.zeros((WIDE - 83, CELLS), F32)], axis=0).astype(BF16)
    spot = lax.broadcasted_iota(jnp.int32, (UNIT, CELLS), 1)
    hot = jnp.where((spot == cell.astype(jnp.int32)) & own, 1.0, 0.0).astype(BF16)
    taken = lax.dot_general(hot, source, (((1,), (1,)), ((), ())), preferred_element_type=F32)
    innov = value - (taken[:, 80:81] + taken[:, 81:82] + taken[:, 82:83])
    across = (cell * (1.0 / TY)).astype(jnp.int32).astype(F32)
    obs_x = across + (patch // PROWS * TX).astype(F32)
    obs_y = cell - across * TY + (patch % PROWS * TY).astype(F32)
    lane = lax.broadcasted_iota(jnp.int32, (UNIT, WIDE), 1)
    out = jnp.where(lane < MEMBERS, taken, 0.0)
    for at, item in enumerate([*split3(innov), *split3(var), obs_x, obs_y, lev]):
        out = jnp.where(lane == INNOV + at, item, out)
    out = packed(jnp.where(own, out, 0.0)).astype(BF16)
    for other in range(2 * NLEV):
        out_ref[other] = out


def gathered(patch):
    return (patch & 15) * 8 + ((patch >> 4) & 3) * 2 + (patch >> 6)


GROUP = [(i >> 1) * 16 + (i & 1) * 64 for i in range(8)]


def first_tile(k):
    return (k + 1) * (NOBS // TILE)


def taper_kernel(
    order_hbm,
    first_hbm,
    vert_hbm,
    horiz_hbm,
    cell_hbm,
    lev_hbm,
    out_hbm,
    order_ref,
    first_ref,
    vert_ref,
    horiz_ref,
    cell_ref,
    lev_ref,
    code_ref,
    slots,
    place,
    hot_x,
    hot_y,
    dist,
    tab_x,
    tab_y,
    levw,
    bufs,
    fetched,
    sems,
):
    fetch(
        [
            (order_hbm, order_ref),
            (first_hbm, first_ref),
            (vert_hbm, vert_ref),
            (horiz_hbm, horiz_ref),
            (cell_hbm, cell_ref),
            (lev_hbm, lev_ref),
        ],
        fetched,
    )
    spot = lax.broadcasted_iota(jnp.int32, (8, NPATCH * CAP), 1).astype(F32)
    patch = ((spot + 0.5) * (1.0 / CAP)).astype(jnp.int32)
    cell = cell_ref[...]
    at_x = (patch // PROWS) * TX + cell // TY
    at_y = (patch % PROWS) * TY + cell % TY
    code_ref[...] = (at_x * 1024 + at_y * NLEV + lev_ref[...]).astype(F32)

    for c in range(NPATCH * CAP // WIDE):
        part = slice(c * WIDE, (c + 1) * WIDE)
        slots[part, :] = jnp.concatenate([code_ref[:, part], jnp.zeros((WIDE - 8, WIDE), F32)], axis=0).T

    def compact(k, unused):
        pick = order_ref[k]

        def put(g, unused):
            for step in GROUP:
                p = g + step
                rows = slots[pl.ds(pl.multiple_of(p * CAP, 8), CAP), :]
                place[pl.ds(k * NOBS + first_ref[pick, p], CAP), :] = rows
            return unused

        return lax.fori_loop(0, NPATCH // 8, put, unused)

    lax.fori_loop(0, NBATCH, compact, 0)

    def mark(t, unused):
        here = pl.ds(pl.multiple_of(t * TILE, TILE), TILE)
        rows = place[here, :]
        lane = lax.broadcasted_iota(jnp.int32, (TILE, WIDE), 1)
        code = jnp.sum(jnp.where(lane == order_ref[t], rows, 0.0), axis=1, keepdims=True)
        code = jnp.broadcast_to(code, (TILE, WIDE))
        place[here, :] = code
        codes = code.astype(jnp.int32)
        hot_x[here, :] = hot(codes >> 10, TILE)
        hot_y[here, :] = hot((codes >> 2) & 255, TILE)
        return unused

    def lookup(bins):
        table = jnp.broadcast_to(horizontal(horiz_ref), (bins.shape[0], WIDE))
        parts = [
            jnp.take_along_axis(table, bins[:, j : j + WIDE], axis=1) for j in range(0, bins.shape[1], WIDE)
        ]
        return jnp.concatenate(parts, axis=1)

    one = lax.broadcasted_iota(jnp.int32, (SPAN, SPAN), 0)
    other = lax.broadcasted_iota(jnp.int32, (SPAN, SPAN), 1)
    apart = jnp.abs(one - other)
    for at, bins in enumerate((jnp.minimum(apart, SPAN - apart) // BIN, apart // BIN)):
        value = lookup(bins)
        high = value.astype(BF16)
        dist[2 * at] = high
        dist[2 * at + 1] = (value - high.astype(F32)).astype(BF16)

    def hot(index, rows):
        lane = lax.broadcasted_iota(jnp.int32, (rows, WIDE), 1)
        parts = [jnp.where(index - j == lane, 1.0, 0.0).astype(BF16) for j in range(0, SPAN, WIDE)]
        return jnp.concatenate(parts, axis=1)

    lax.fori_loop(0, LIVE_COLS // TILE, mark, 0)

    def out_copy(n):
        return pltpu.make_async_copy(bufs.at[n % 2], out_hbm.at[n], sems.at[n % 2])

    def batch(k, n):
        rows = pl.ds(pl.multiple_of(k * NOBS, NOBS), NOBS)
        obs_z = place[rows, :].T[:1].astype(jnp.int32) & 3
        lane = lax.broadcasted_iota(jnp.int32, (1, NOBS), 1)
        vary = 1.0 + (lane & 63).astype(F32) * (1.0 / 64.0)
        contract = (((1,), (1,)), ((), ()))
        for tab, hot_rows, at, factor in ((tab_x, hot_x, 0, vary), (tab_y, hot_y, 2, 1.0 / vary)):
            here = hot_rows[rows, :]
            full = lax.dot_general(dist[at], here, contract, preferred_element_type=F32)
            full = full + lax.dot_general(dist[at + 1], here, contract, preferred_element_type=F32)
            tab[...] = (full * factor).astype(BF16)
        for z in range(NLEV):
            apart = jnp.abs(obs_z - z)
            found = jnp.zeros((1, NOBS), F32)
            for step in range(NLEV):
                found = jnp.where(apart == step, vert_ref[step], found)
            levw[z : z + 1, :] = found

        def tile(t, n):
            here = pl.ds(pl.multiple_of(t * TILE, TILE), TILE)
            lhs_x = hot_x[here, :]
            lhs_y = hot_y[here, :]
            cell_z = place[here, :].astype(jnp.int32) & 3
            cell_z = jnp.concatenate([cell_z, cell_z], axis=1)

            @pl.when(n >= 2)
            def _():
                out_copy(n - 2).wait()

            buf = bufs.at[n % 2]
            for j in range(0, NOBS, SPAN):
                part = slice(j, j + SPAN)
                near = jnp.dot(lhs_x, tab_x[:, part], preferred_element_type=F32)
                far = jnp.dot(lhs_y, tab_y[:, part], preferred_element_type=F32)
                low = jnp.where(cell_z == 0, levw[0:1, part], levw[1:2, part])
                high = jnp.where(cell_z == 2, levw[2:3, part], levw[3:4, part])
                buf[:, part] = (near * far * jnp.where(cell_z < 2, low, high)).astype(BF16)
            out_copy(n).start()
            return n + 1

        return lax.fori_loop(first_tile(k), LIVE_COLS // TILE, tile, n)

    total = lax.fori_loop(0, NBATCH - 1, batch, 0)
    out_copy(total - 2).wait()
    out_copy(total - 1).wait()


def filter_kernel(
    where_ref,
    order_hbm,
    first_hbm,
    vert_hbm,
    horiz_hbm,
    got_hbm,
    pert_hbm,
    mean_hbm,
    taper_hbm,
    post_pert_hbm,
    post_mean_ref,
    order_ref,
    first_ref,
    vert_ref,
    horiz_ref,
    got_ref,
    pert_ref,
    mean_ref,
    state,
    prior,
    coeffs,
    lines,
    gain,
    bufs,
    fetched,
    arrived,
    sems,
):
    patch = where_ref[0]
    level = where_ref[1].astype(F32)

    def taper_copy(n):
        return pltpu.make_async_copy(taper_hbm.at[n], bufs.at[n % 2], sems.at[n % 2])

    def part_copy(c):
        rows = pl.ds(c * (NPATCH * PACK // PARTS), NPATCH * PACK // PARTS)
        return pltpu.make_async_copy(got_hbm.at[rows, :], got_ref.at[rows, :], arrived.at[c])

    for c in range(PARTS):
        part_copy(c).start()
    fetch(
        [
            (order_hbm, order_ref),
            (first_hbm, first_ref),
            (vert_hbm, vert_ref),
            (horiz_hbm, horiz_ref),
            (pert_hbm.at[:, 0, :], pert_ref),
            (mean_hbm, mean_ref),
        ],
        fetched,
    )
    taper_copy(0).start()
    own = jnp.concatenate(
        [pert_ref[...], -mean_ref[...], jnp.zeros((WIDE - 81, CELLS), F32)], axis=0
    )
    state[OWN : OWN + CELLS, :] = own.T

    def place(g, unused):
        for i, step in enumerate(GROUP):
            at = pl.multiple_of(g * (8 * PACK) + i * PACK, 16)
            for k, rows in enumerate(unpacked(got_ref[pl.ds(at, PACK), :].astype(F32))):
                first = first_ref[order_ref[k], g + step]
                state[pl.ds(k * SLAB + first, CAP), :] = rows
        return unused

    for c in range(PARTS):
        part_copy(c).wait()
        lax.fori_loop(c * (16 // PARTS), (c + 1) * (16 // PARTS), place, 0)

    def lookup(bins):
        table = jnp.broadcast_to(horizontal(horiz_ref), (bins.shape[0], WIDE))
        parts = [
            jnp.take_along_axis(table, bins[:, j : j + WIDE], axis=1) for j in range(0, bins.shape[1], WIDE)
        ]
        return jnp.concatenate(parts, axis=1)

    def bins_x(one, other):
        apart = jnp.abs(one - other)
        return (jnp.minimum(apart, SPAN - apart) * (1.0 / BIN)).astype(jnp.int32)

    def bins_y(one, other):
        return (jnp.abs(one - other) * (1.0 / BIN)).astype(jnp.int32)

    def vertical(apart):
        found = jnp.zeros_like(apart)
        for step in range(NLEV):
            found = jnp.where(apart == float(step), vert_ref[step], found)
        return found

    def slab(k):
        return pl.ds(pl.multiple_of(k * SLAB, 32), NOBS)

    def prepare(k, slot):
        block = state[slab(k), :].T
        innov = block[INNOV : INNOV + 1] + block[INNOV + 1 : INNOV + 2] + block[INNOV + 2 : INNOV + 3]
        obs_var = block[VAR : VAR + 1] + block[VAR + 1 : VAR + 2] + block[VAR + 2 : VAR + 3]
        row = lax.broadcasted_iota(jnp.int32, (WIDE, NOBS), 0)
        rounded = jnp.where(row < MEMBERS, block, 0.0).astype(BF16)
        values = rounded.astype(F32)
        spread = jnp.sum(values * values, axis=0, keepdims=True) / (MEMBERS - 1.0) + obs_var
        shrink = 1.0 / (1.0 + jnp.sqrt(obs_var / spread))
        prior[slot] = rounded
        lines[slot, 0:1] = 1.0 / ((MEMBERS - 1.0) * spread)
        lines[slot, 1:4] = block[POS_X : POS_Z + 1]
        coeffs[slot] = jnp.where(row == MEMBERS, innov.astype(BF16).astype(F32), values * shrink).T.astype(BF16)

    def own_update(slot, cells):
        scale, obs_x = lines[slot, 0:1], lines[slot, 1:2]
        obs_y, obs_z = lines[slot, 2:3], lines[slot, 3:4]
        own_a = lax.broadcasted_iota(jnp.int32, (TX, NOBS), 0) + patch // PROWS * TX
        own_e = lax.broadcasted_iota(jnp.int32, (TY, NOBS), 0) + patch % PROWS * TY
        weight_x = lookup(bins_x(own_a.astype(F32), obs_x)) * (vertical(jnp.abs(obs_z - level)) * scale)
        weight_y = lookup(bins_y(own_e.astype(F32), obs_y))
        lhs = cells.astype(BF16)
        change = jnp.zeros((CELLS, WIDE), F32)
        for j in range(0, NOBS, SPAN):
            part = slice(j, j + SPAN)
            cov = jnp.dot(lhs, prior[slot, :, part], preferred_element_type=F32)
            mixed = jnp.concatenate(
                [
                    (cov[a * TY : (a + 1) * TY] * (weight_x[a : a + 1, part] * weight_y[:, part])).astype(BF16)
                    for a in range(TX)
                ],
                axis=0,
            )
            change = change + jnp.dot(mixed, coeffs[slot, part], preferred_element_type=F32)
        return cells - change

    def pair_update(slot, cells, n):
        scale = lines[slot, 0:1]
        lhs = cells.astype(BF16)
        taper = bufs.at[n % 2]
        for j in range(0, NOBS, SPAN):
            part = slice(j, j + SPAN)
            cov = jnp.dot(lhs, prior[slot, :, part], preferred_element_type=F32)
            gain[:, part] = taper[:, part] * (cov * scale[:, part]).astype(BF16)
        return cells - jnp.dot(gain[...], coeffs[slot], preferred_element_type=F32)

    def next_taper(n):
        taper_copy(n).wait()

        @pl.when(n < NTILES - 1)
        def _():
            taper_copy(n + 1).start()

    def own_and_first(k, slot, n):
        next_taper(n)
        mine, first = state[OWN : OWN + CELLS, :], state[slab(k + 1), :]
        mine, first = own_update(slot, mine), pair_update(slot, first, n)
        state[OWN : OWN + CELLS, :] = mine
        state[slab(k + 1), :] = first

    def batch(k, slot, n):
        own_and_first(k, slot, n)
        next_taper(n + 1)
        cells = state[slab(k + 2), :]
        prepare(k + 1, 1 - slot)
        state[slab(k + 2), :] = pair_update(slot, cells, n + 1)

        def tile(t, n):
            next_taper(n)
            state[slab(t), :] = pair_update(slot, state[slab(t), :], n)
            return n + 1

        return lax.fori_loop(k + 3, NBATCH, tile, n + 2)

    def two(i, n):
        return batch(2 * i + 1, 1, batch(2 * i, 0, n))

    prepare(0, 0)
    total = lax.fori_loop(0, NBATCH // 2 - 1, two, 0)
    own_and_first(NBATCH - 2, 0, total)
    prepare(NBATCH - 1, 1)
    state[OWN : OWN + CELLS, :] = own_update(1, state[OWN : OWN + CELLS, :])
    block = state[OWN : OWN + CELLS, :].T
    pert_ref[...] = block[:MEMBERS]
    post_mean_ref[...] = -block[MEMBERS : MEMBERS + 1]
    fetch([(pert_ref, post_pert_hbm.at[:, 0, :])], fetched)


HBM = pltpu.HBM
DMA = pltpu.SemaphoreType.DMA
GRANT = pltpu.CompilerParams(vmem_limit_bytes=60 << 20)


def spec(space):
    return pl.BlockSpec(memory_space=space)


def select_call(where, order, count, cell, lev, value, var, mean, pert):
    return pl.pallas_call(
        select_kernel,
        out_shape=(
            jax.ShapeDtypeStruct((2 * NLEV, PACK, WIDE), BF16),
            jax.ShapeDtypeStruct((8, NPATCH), jnp.int32),
        ),
        in_specs=[spec(SMEM)] + [spec(HBM)] * 8,
        out_specs=(spec(VMEM),) * 2,
        scratch_shapes=[
            SMEM((8,), jnp.int32),
            SMEM((8, NPATCH), jnp.int32),
            VMEM((8, NPATCH), jnp.int32),
            VMEM((8, 2 * WIDE), jnp.int32),
            VMEM((8, 2 * WIDE), jnp.int32),
            VMEM((8, 2 * WIDE), F32),
            VMEM((8, 2 * WIDE), F32),
            VMEM((1, CELLS), F32),
            VMEM((MEMBERS, CELLS), F32),
            DMA((9,)),
        ],
        compiler_params=GRANT,
    )(where, order, count, cell, lev, value, var, mean, pert)


def taper_call(order, first, vert, horiz, cell, lev):
    return pl.pallas_call(
        taper_kernel,
        out_shape=jax.ShapeDtypeStruct((NTILES, TILE, NOBS), BF16),
        in_specs=[spec(HBM)] * 6,
        out_specs=spec(HBM),
        scratch_shapes=[
            SMEM((8,), jnp.int32),
            SMEM((8, NPATCH), jnp.int32),
            SMEM((NLEV,), F32),
            SMEM((NBIN,), F32),
            VMEM((8, NPATCH * CAP), jnp.int32),
            VMEM((8, NPATCH * CAP), jnp.int32),
            VMEM((8, NPATCH * CAP), F32),
            VMEM((NPATCH * CAP, WIDE), F32),
            VMEM((LIVE_COLS + 2 * CAP, WIDE), F32),
            VMEM((LIVE_COLS, SPAN), BF16),
            VMEM((LIVE_COLS, SPAN), BF16),
            VMEM((4, SPAN, SPAN), BF16),
            VMEM((SPAN, NOBS), BF16),
            VMEM((SPAN, NOBS), BF16),
            VMEM((8, NOBS), F32),
            VMEM((2, TILE, NOBS), BF16),
            DMA((6,)),
            DMA((2,)),
        ],
        compiler_params=GRANT,
        cost_estimate=pl.CostEstimate(flops=2 * 15 * NOBS * NOBS * 512, bytes_accessed=32 << 20, transcendentals=0),
    )(order, first, vert, horiz, cell, lev)


def filter_call(where, order, first, vert, horiz, got, pert, mean, taper):
    return pl.pallas_call(
        filter_kernel,
        out_shape=(
            jax.ShapeDtypeStruct((MEMBERS, 1, CELLS), F32),
            jax.ShapeDtypeStruct((1, CELLS), F32),
        ),
        in_specs=[spec(SMEM)] + [spec(HBM)] * 8,
        out_specs=(spec(HBM), spec(VMEM)),
        scratch_shapes=[
            SMEM((8,), jnp.int32),
            SMEM((8, NPATCH), jnp.int32),
            SMEM((NLEV,), F32),
            SMEM((NBIN,), F32),
            VMEM((NPATCH * PACK, WIDE), BF16),
            VMEM((MEMBERS, CELLS), F32),
            VMEM((1, CELLS), F32),
            VMEM((OWN + CELLS, WIDE), F32),
            VMEM((2, WIDE, NOBS), BF16),
            VMEM((2, NOBS, WIDE), BF16),
            VMEM((2, 8, NOBS), F32),
            VMEM((TILE, NOBS), BF16),
            VMEM((2, TILE, NOBS), BF16),
            DMA((6,)),
            DMA((PARTS,)),
            DMA((2,)),
        ],
        compiler_params=GRANT,
    )(where, order, first, vert, horiz, got, pert, mean, taper)


def exchange(block, axes):
    return lax.all_to_all(block, axes, 0, 0)


AXES = ("y_hi", "x", "z", "core")


def shards(
    prior_mean,
    prior_pert,
    obs_value,
    obs_var,
    obs_cell,
    obs_level,
    obs_count,
    batch_order,
    horiz_weight,
    vert_weight,
):
    where = jnp.stack([lax.axis_index(AXES), lax.axis_index("y_lo")]).astype(jnp.int32)
    mean = prior_mean
    mine, first = select_call(
        where, batch_order, obs_count, obs_cell, obs_level, obs_value, obs_var, mean, prior_pert
    )
    ring = exchange(mine, ("y_hi", "y_lo")).reshape(2, NLEV, PACK, WIDE)
    pair = jnp.sum(ring.astype(F32), axis=1).astype(BF16).reshape(1, 2 * PACK, WIDE)
    group = exchange(jnp.broadcast_to(pair, (4, 2 * PACK, WIDE)), "x").reshape(8 * PACK, WIDE)
    group, first = lax.optimization_barrier((group, first))
    got = lax.all_gather(group, ("z", "core"), axis=0, tiled=True)
    taper = taper_call(batch_order, first, vert_weight, horiz_weight, obs_cell, obs_level)
    post_pert, post_mean = filter_call(
        where, batch_order, first, vert_weight, horiz_weight, got, prior_pert, mean, taper
    )
    return post_mean, post_pert


def solution(mesh):
    whole = Mesh(mesh.devices.reshape(2, 4, 8, 2, NLEV), AXES + ("y_lo",))
    return jax.shard_map(
        shards,
        mesh=whole,
        in_specs=(
            P("y_lo", AXES),
            P(None, "y_lo", AXES),
            P(),
            P(),
            P(),
            P(),
            P(),
            P(),
            P(),
            P(),
        ),
        out_specs=(P("y_lo", AXES), P(None, "y_lo", AXES)),
        check_vma=False,
    )
```
